256 devices in a mesh: order: 16 (over z_hi, y, core), chan: 16 (over x, z_lo).
Axes of the slice: x: 4, y: 4, z: 8 (z_hi: 2, z_lo: 4; z = z_hi * 4 + z_lo), core: 2. Of those that a mesh axis runs over, the one named last changes fastest.
Arguments:
- window: int32 [1], replicated, may hold values from 0 to 712
- inputs: bfloat16 [2, 2, 8, 720, 2048], P(None, None, None, 'order', 'chan'), may hold values from -6 to 6
- out_grad: bfloat16 [2, 2, 8, 720, 2048], P(None, None, None, 'order', 'chan'), may hold values from -6 to 6
- weights: bfloat16 [2, 16384, 2048], P(None, None, 'chan'), may hold values from -0.1875 to 0.1875
Outputs:
- in_grad: float32 [2, 2, 8, 720, 2048], P(None, None, None, 'order', 'chan')
- weight_grad: float32 [2, 16384, 2048], P(None, 'order', 'chan')
The draws below stay inside these ranges and needn't reach their ends.
Inputs may be any that keep to these rules, and one draw needn't show every extreme that they name: window[0] + 8 <= 720.
All inputs are finite; a program needn't handle non-finite values.
Results may differ from the reference program's by a relative error of at most 0.0003.
Values may be sent and summed in bfloat16 or wider, within the bound.
A program may use at most 128 MiB of HBM per device.

```python
import jax
import jax.numpy as jnp

CH = 2048
LMAX = 720
LWIN = 8
BATCH = 2


def raised(result, own_key, source, target, parts, factor):
    owner, partner = [(jnp.arange(result.shape[axis_at]) // (result.shape[axis_at] // parts)).reshape([-1 if axis == axis_at else 1 for axis in range(result.ndim)]) for axis_at in (source, target)]
    chosen = jax.random.permutation(own_key, parts)[partner]
    strong = (owner == chosen) | (owner == (partner + parts // 2) % parts)
    return jnp.where(strong, factor * result, result)


def block_scale(own_key, dims, split, low, high):
    def one(axis_at, parts):
        draws = jax.random.uniform(jax.random.fold_in(jax.random.fold_in(own_key, 6), axis_at), (parts,), jnp.float32, low / len(split), high / len(split))
        return jnp.repeat(jnp.exp(draws), dims[axis_at] // parts).reshape((-1,) + (1,) * (len(dims) - axis_at - 1))

    factor_of = one(*split[0])
    for cut in split[1:]:
        factor_of = factor_of * one(*cut)
    return factor_of


def scatter_about(own_key, dims, deviation, bound, pieces=(), held_as=jnp.bfloat16):
    array = deviation * jax.random.normal(own_key, dims, jnp.float32)
    if pieces:
        array = array * block_scale(own_key, dims, pieces, -0.22, 0.18)
    return jnp.clip(array, -bound, bound).astype(held_as)


def bell_draw_with(own_key, dims, deviation, reach, cuts, heavy, kind=jnp.bfloat16):
    values = deviation * jax.random.normal(own_key, dims, jnp.float32)
    if cuts:
        values = values * block_scale(own_key, dims, cuts, -0.22, 0.18)
    return jnp.clip(raised(values, jax.random.fold_in(own_key, 3), *heavy), -reach, reach).astype(kind)


def setup_inputs(seed: int = 0) -> dict:
    key_list = jax.random.split(jax.random.key(seed), 5)
    return {
        "window": jax.random.randint(key_list[0], (1,), 0, LMAX - LWIN + 1).astype(jnp.int32),
        "inputs": bell_draw_with(key_list[1], (2, BATCH, LWIN, LMAX, CH), 1.0, 6.0, ((3, 16), (4, 16)), (3, 4, 16, 2.0)),
        "out_grad": scatter_about(key_list[2], (2, BATCH, LWIN, LMAX, CH), 1.0, 6.0, ((3, 16), (4, 16))),
        "weights": bell_draw_with(key_list[3], (2, LWIN * CH, CH), CH ** -0.5, 0.1875, ((2, 16),), (2, 1, 16, 2.0)),
    }


def reference(window, inputs, out_grad, weights):
    degrees = window[0] + jnp.arange(LWIN, dtype=jnp.int32)
    orders = jnp.arange(LMAX, dtype=jnp.int32)
    live_mask = (orders[None, :] <= degrees[:, None]).astype(jnp.bfloat16)[:, :, None]
    masked_in = (inputs * live_mask).astype(jnp.float32)
    masked_grad = (out_grad * live_mask).astype(jnp.float32)
    mixing = weights.astype(jnp.float32).reshape(2, LWIN, CH, CH)
    grad_re, grad_im = masked_grad[0], masked_grad[1]
    mix_re, mix_im = mixing[0], mixing[1]
    back_re = jnp.einsum('blmo,lio->blmi', grad_re, mix_re) + jnp.einsum('blmo,lio->blmi', grad_im, mix_im)
    back_im = jnp.einsum('blmo,lio->blmi', grad_im, mix_re) - jnp.einsum('blmo,lio->blmi', grad_re, mix_im)
    in_grad = jnp.stack([back_re, back_im])
    input_re, input_im = masked_in[0], masked_in[1]
    wgrad_re = jnp.einsum('blmi,blmo->lio', input_re, grad_re) + jnp.einsum('blmi,blmo->lio', input_im, grad_im)
    wgrad_im = jnp.einsum('blmi,blmo->lio', input_re, grad_im) - jnp.einsum('blmi,blmo->lio', input_im, grad_re)
    weight_grad = jnp.stack([wgrad_re, wgrad_im]).reshape(2, LWIN * CH, CH)
    return in_grad, weight_grad
```

```python
import functools

import jax
import jax.numpy as jnp
from jax import lax
from jax.experimental import pallas as pl
from jax.experimental.pallas import tpu as pltpu
from jax.sharding import PartitionSpec as P

MESH = pl.DeviceIdType.MESH
BF16, F32 = jnp.bfloat16, jnp.float32

NX, NY, NZ = 4, 4, 4
NB = 8


def coords():
    order, chan = lax.axis_index("order"), lax.axis_index("chan")
    return order // 8, (order // 2) % 4, order % 2, chan // 4, chan % 4


def lanes(block):
    return pl.ds(pl.multiple_of(block * 128, 128), 128)


def kernel(
    rows, x_ref, g_ref, w_ref, back_ref, wgrad_ref,
    xz, gx, gz, wt, acc, pair, part, heap, fin, ret, wg,
    xa_s, xa_r, ga_s, ga_r, gi_s, gi_r, w_s, w_r, w_loc,
    xr_s, xl_s, xz_r, gr_s, gl_s, gz_r, gx_s, gx_r,
    pair_s, pair_r, wo_s, wo_r, rs_s, rs_r, rt_s, rt_r, out_s,
):
    zh, y, k, x, zl = coords()
    z = zh * 4 + zl
    half = rows // 2
    me = y * 2 + k

    def dev(zh_, y_, k_, x_, zl_):
        return (zh_ * 8 + y_ * 2 + k_, x_ * 4 + zl_)

    def at_z(z_):
        return dev(z_ // 4, y, k, x, z_ % 4)

    def greet(device):
        pl.semaphore_signal(pltpu.get_barrier_semaphore(), inc=1, device_id=device, device_id_type=MESH)

    def greet_order(t, _):
        other = (zh * 8 + me + t) % 16
        greet((other, x * 4 + zl))
        return 0

    lax.fori_loop(1, 16, greet_order, 0)
    for d in (1, 2, 3, 5, 6, 7):
        greet(at_z((z + d) % 8))
    for d in (1, 2, 3):
        for other in (0, 1):
            greet(dev(zh, y, other, (x + d) % 4, zl))
    pl.semaphore_wait(pltpu.get_barrier_semaphore(), 15 + 6 + 6)

    def remote(src, dst, send, recv, device):
        return pltpu.make_async_remote_copy(
            src_ref=src, dst_ref=dst, send_sem=send, recv_sem=recv, device_id=device, device_id_type=MESH
        )

    def blk(buf, b, lane):
        return buf.at[b, :, lanes(lane)]

    def to_weight(src, buf, lane, send, recv, t):
        e = (zh * 4 + y + t) % 8
        remote(src.at[e], blk(buf, me, lane), send.at[e], recv.at[me], dev(e // 4, e % 4, zh, x, zl)).start()

    def own_weight(src, buf, lane, recv, e):
        pltpu.make_async_copy(src.at[e], blk(buf, me, lane), recv.at[me]).start()

    def weight_out(src, buf, lane, send, recv):
        mine = zh == k

        @pl.when(mine)
        def _():
            own_weight(src, buf, lane, recv, zh * 4 + y)

        @pl.when(jnp.logical_not(mine))
        def _():
            to_weight(src, buf, lane, send, recv, 0)

        def step(t, _):
            to_weight(src, buf, lane, send, recv, t)
            return 0

        lax.fori_loop(1, 8, step, 0)

    def to_input(t):
        j = (me + t) % 8
        y_, k_ = j // 2, j % 2
        return remote(g_ref.at[4 * k_ + y_], blk(gz, me, zl), gi_s.at[j], gi_r.at[me], dev(zh, y_, k_, x, zl))

    weight_out(x_ref, xz, zl, xa_s, xa_r)
    weight_out(g_ref, gx, x, ga_s, ga_r)

    degree = 4 * k + y
    w_loc_copy = pltpu.make_async_copy(w_ref.at[:, degree, :, zl], wt.at[:, :, :, lanes(zl)], w_loc)
    w_loc_copy.start()
    w_copies = []
    for i, (d, part_of) in enumerate(((1, (0, 2)), (7, (0, 2)), (2, (0, 1)), (6, (1, 1)))):
        to = (z + d) % 8
        reim = pl.ds(*part_of)
        w_copies.append(
            remote(w_ref.at[reim, degree, :, to % 4], wt.at[reim, :, :, lanes(zl)], w_s.at[i], w_r.at[i], at_z(to))
        )
        w_copies[-1].start()

    def gi_step(t, _):
        to_input(t).start()
        return 0

    lax.fori_loop(1, 8, gi_step, 0)
    pltpu.make_async_copy(g_ref.at[degree], blk(gz, me, zl), gi_r.at[me]).start()

    def right(buf, o, b, send, recv):
        return remote(blk(buf, b, o), blk(buf, b, o), send.at[o, b], recv.at[o, b], dev(zh, y, k, x, (zl + 1) % 4))

    def left(buf, o, b, send, recv):
        return remote(blk(buf, b, o), blk(buf, b, o), send.at[o, b], recv.at[o, b], dev(zh, y, k, x, (zl + 3) % 4))

    def own_line(buf, b, s_r, s_l, recv):
        @pl.when(zl < 3)
        def _():
            right(buf, zl, b, s_r, recv).start()

        @pl.when(zl > 0)
        def _():
            left(buf, zl, b, s_l, recv).start()

    def pass_line(buf, b, d, s_r, s_l, recv):
        @pl.when(zl >= d)
        def _():
            o = zl - d
            right(buf, o, b, s_r, recv).wait_recv()

            @pl.when(zl < 3)
            def _():
                right(buf, o, b, s_r, recv).start()

        @pl.when(zl + d <= 3)
        def _():
            o = zl + d
            left(buf, o, b, s_l, recv).wait_recv()

            @pl.when(zl > 0)
            def _():
                left(buf, o, b, s_l, recv).start()

    def drain_line(buf, b, s_r, s_l, recv):
        for d in range(3):
            @pl.when((zl >= d) & (zl < 3))
            def _():
                right(buf, zl - d, b, s_r, recv).wait_send()

            @pl.when((zl + d <= 3) & (zl > 0))
            def _():
                left(buf, zl + d, b, s_l, recv).wait_send()

    def ring(d, b):
        return remote(blk(gx, b, x), blk(gx, b, x), gx_s.at[d, b], gx_r.at[d, b], dev(zh, y, k, (x + d) % 4, zl))

    def first(b, _):
        pltpu.make_async_copy(x_ref.at[0], blk(xz, b, zl), xa_r.at[b]).wait()
        own_line(xz, b, xr_s, xl_s, xz_r)
        pltpu.make_async_copy(g_ref.at[0], blk(gx, b, x), ga_r.at[b]).wait()
        for d in (1, 3, 2):
            ring(d, b).start()
        return 0

    lax.fori_loop(0, NB, first, 0)

    def second(b, _):
        pltpu.make_async_copy(g_ref.at[0], blk(gz, b, zl), gi_r.at[b]).wait()
        own_line(gz, b, gr_s, gl_s, gz_r)
        return 0

    lax.fori_loop(0, NB, second, 0)

    def pass_x(d):
        def step(b, _):
            pass_line(xz, b, d, xr_s, xl_s, xz_r)
            return 0

        lax.fori_loop(0, NB, step, 0)

    def pass_g(d):
        def step(b, _):
            pass_line(gz, b, d, gr_s, gl_s, gz_r)
            return 0

        lax.fori_loop(0, NB, step, 0)

    pass_x(1)
    pass_g(1)
    pass_x(2)

    acc[...] = jnp.zeros_like(acc)

    def wgrad_step(c, _):
        for j in range(2):
            b = 2 * c + j
            pass_line(xz, b, 3, xr_s, xl_s, xz_r)
            for d in (1, 2, 3):
                remote(
                    blk(gx, b, x), blk(gx, b, (x + 4 - d) % 4), gx_s.at[d, b], gx_r.at[d, b],
                    dev(zh, y, k, (x + d) % 4, zl),
                ).wait_recv()
        left_ = xz[pl.ds(2 * c, 2)].reshape(2 * rows, 512)
        right_ = gx[pl.ds(2 * c, 2)]
        turned = jnp.concatenate([right_[:, half:], -right_[:, :half]], axis=1).reshape(2 * rows, 512)
        right_ = right_.reshape(2 * rows, 512)
        over_rows = (((0,), (0,)), ((), ()))
        acc[0] += lax.dot_general(left_, right_, over_rows, preferred_element_type=F32)
        acc[1] += lax.dot_general(left_, turned, over_rows, preferred_element_type=F32)
        return 0

    lax.fori_loop(0, NB // 2, wgrad_step, 0)

    swap = remote(acc.at[1 - k], pair, pair_s, pair_r, dev(zh, y, 1 - k, x, zl))
    swap.start()
    pass_g(2)
    swap.wait_recv()
    acc[k] = acc[k] + pair[...]

    def wgrad_to(d):
        return remote(
            acc.at[k, :, lanes((x + d) % 4)],
            wg.at[k, pl.ds(pl.multiple_of((x % 2) * 512, 512), 512)],
            wo_s.at[d], wo_r.at[x % 2, k], dev(zh, y, x // 2, (x + d) % 4, zl),
        )

    for d in (1, 3, 2):
        wgrad_to(d).start()

    @pl.when(k == x // 2)
    def _():
        pltpu.make_async_copy(
            acc.at[k, :, lanes(x)], wg.at[k, pl.ds(pl.multiple_of((x % 2) * 512, 512), 512)], wo_r.at[x % 2, k]
        ).start()

    @pl.when(k != x // 2)
    def _():
        wgrad_to(0).start()

    w_loc_copy.wait()
    for copy in w_copies:
        copy.wait_recv()

    def scatter(d, c):
        x_ = (x + d) % 4
        return remote(
            part.at[x_, pl.ds(2 * c, 2)], heap.at[d - 1, pl.ds(2 * c, 2)], rs_s.at[d - 1, c], rs_r.at[d - 1, c],
            dev(zh, y, k, x_, zl),
        )

    def home(b):
        y_, k_ = b // 2, b % 2
        return remote(fin.at[b], ret.at[degree], rt_s.at[b], rt_r.at[degree], dev(zh, y_, k_, x, zl))

    def reduce_step(c):
        for d in (1, 2, 3):
            scatter(d, c).wait_recv()
        for j in range(2):
            b = 2 * c + j
            fin[b] = (part[x, b] + heap[0, b]) + (heap[1, b] + heap[2, b])

            @pl.when(b == me)
            def _():
                pltpu.make_async_copy(fin.at[b], ret.at[degree], rt_r.at[degree]).start()

            @pl.when(b != me)
            def _():
                home(b).start()

    def back_step(c, _):
        for j in range(2):
            pass_line(gz, 2 * c + j, 3, gr_s, gl_s, gz_r)
        cot = gz[pl.ds(2 * c, 2)].reshape(2 * rows, 512)
        over_lanes = (((1,), (1,)), ((), ()))
        by_re = lax.dot_general(cot, wt[0].reshape(512, 512), over_lanes, preferred_element_type=F32)
        by_im = lax.dot_general(cot, wt[1].reshape(512, 512), over_lanes, preferred_element_type=F32)
        for j in range(2):
            lo, mid, hi = j * rows, j * rows + half, (j + 1) * rows
            back_re = by_re[lo:mid] + by_im[mid:hi]
            back_im = by_re[mid:hi] - by_im[lo:mid]
            for x_ in range(NX):
                part[x_, 2 * c + j, 0:half] = back_re[:, x_ * 128 : (x_ + 1) * 128]
                part[x_, 2 * c + j, half:rows] = back_im[:, x_ * 128 : (x_ + 1) * 128]
        for d in (1, 3, 2):
            scatter(d, c).start()

        @pl.when(c > 0)
        def _():
            reduce_step(c - 1)

        return 0

    lax.fori_loop(0, NB // 2, back_step, 0)
    reduce_step(NB // 2 - 1)

    for r in range(2):
        for k_ in range(2):
            pltpu.make_async_copy(
                acc.at[0, :, pl.ds(0, 128)], wg.at[k_, pl.ds(r * 512, 512)], wo_r.at[r, k_]
            ).wait()
    wg_out = pltpu.make_async_copy(wg, wgrad_ref, out_s.at[0])
    wg_out.start()

    def returned(l, _):
        pltpu.make_async_copy(fin.at[0], ret.at[l], rt_r.at[l]).wait()
        return 0

    lax.fori_loop(0, NB, returned, 0)
    back_out = pltpu.make_async_copy(ret, back_ref, out_s.at[1])
    back_out.start()

    def drain(b, _):
        drain_line(xz, b, xr_s, xl_s, xz_r)
        drain_line(gz, b, gr_s, gl_s, gz_r)
        for d in (1, 2, 3):
            ring(d, b).wait_send()

        @pl.when(jnp.logical_or(zh != k, b != zh * 4 + y))
        def _():
            pltpu.make_async_copy(x_ref.at[b], blk(xz, 0, zl), xa_s.at[b]).wait()
            pltpu.make_async_copy(g_ref.at[b], blk(gx, 0, x), ga_s.at[b]).wait()

        @pl.when(b != me)
        def _():
            pltpu.make_async_copy(g_ref.at[0], blk(gz, 0, zl), gi_s.at[b]).wait()
            home(b).wait_send()

        return 0

    lax.fori_loop(0, NB, drain, 0)

    def drain_scatter(c, _):
        for d in (1, 2, 3):
            scatter(d, c).wait_send()
        return 0

    lax.fori_loop(0, NB // 2, drain_scatter, 0)
    for copy in w_copies:
        copy.wait_send()
    swap.wait_send()
    for d in (1, 2, 3):
        wgrad_to(d).wait_send()

    @pl.when(k != x // 2)
    def _():
        wgrad_to(0).wait_send()

    wg_out.wait()
    back_out.wait()


def per_device(window, inputs, out_grad, weights):
    _, samples, degrees, orders, width = inputs.shape
    first_order = lax.axis_index("order") * orders
    degree = window[0] + jnp.arange(degrees, dtype=jnp.int32)
    order = first_order + jnp.arange(orders, dtype=jnp.int32)
    live = (order[None, :] <= degree[:, None]).astype(BF16)[:, :, None]
    real = samples * orders
    half = -(-real // 16) * 16
    rows = 2 * half

    def by_degree(a):
        a = (a * live).transpose(2, 0, 1, 3, 4).reshape(degrees, 2, real, width)
        return jnp.pad(a, ((0, 0), (0, 0), (0, half - real), (0, 0))).reshape(degrees, rows, width)

    dma, vmem = pltpu.SemaphoreType.DMA, pltpu.VMEM
    back, wgrad = pl.pallas_call(
        functools.partial(kernel, rows),
        name="mix_back",
        out_shape=(
            jax.ShapeDtypeStruct((degrees, rows, width), F32),
            jax.ShapeDtypeStruct((2, 1024, width), F32),
        ),
        in_specs=[
            pl.BlockSpec(memory_space=pltpu.VMEM),
            pl.BlockSpec(memory_space=pltpu.VMEM),
            pl.BlockSpec(memory_space=pl.ANY),
        ],
        out_specs=(pl.BlockSpec(memory_space=pl.ANY), pl.BlockSpec(memory_space=pl.ANY)),
        scratch_shapes=[
            vmem((NB, rows, 512), BF16),
            vmem((NB, rows, 512), BF16),
            vmem((NB, rows, 512), BF16),
            vmem((2, 4, 128, 512), BF16),
            vmem((2, 512, 512), F32),
            vmem((512, 512), F32),
            vmem((NX, NB, rows, 128), F32),
            vmem((3, NB, rows, 128), F32),
            vmem((NB, rows, 128), F32),
            vmem((NB, rows, 128), F32),
            vmem((2, 1024, 128), F32),
            dma((8,)), dma((8,)), dma((8,)), dma((8,)), dma((8,)), dma((8,)), dma((4,)), dma((4,)), dma(()),
            dma((4, 8)), dma((4, 8)), dma((4, 8)), dma((4, 8)), dma((4, 8)), dma((4, 8)), dma((4, 8)), dma((4, 8)),
            dma(()), dma(()), dma((4,)), dma((2, 2)), dma((3, 4)), dma((3, 4)), dma((8,)), dma((8,)), dma((2,)),
        ],
        compiler_params=pltpu.CompilerParams(
            collective_id=0, has_side_effects=True, vmem_limit_bytes=44 * 2**20
        ),
    )(by_degree(inputs), by_degree(out_grad), weights.reshape(2, degrees, 4, 4, 128, width))
    back = back.reshape(degrees, 2, half, width)[:, :, :real].reshape(degrees, 2, samples, orders, width)
    return back.transpose(1, 2, 0, 3, 4), wgrad


def solution(mesh):
    placed = (
        P(),
        P(None, None, None, "order", "chan"),
        P(None, None, None, "order", "chan"),
        P(None, None, "chan"),
    )
    return jax.shard_map(
        per_device,
        mesh=mesh,
        in_specs=placed,
        out_specs=(P(None, None, None, "order", "chan"), P(None, "order", "chan")),
        check_vma=False,
    )
```

```python
import functools

import jax
import jax.numpy as jnp
from jax import lax
from jax.experimental import pallas as pl
from jax.experimental.pallas import tpu as pltpu
from jax.sharding import PartitionSpec as P

MESH = pl.DeviceIdType.MESH
BF16, F32 = jnp.bfloat16, jnp.float32

NX, NY, NZ = 4, 4, 4
NB = 8


def coords():
    order, chan = lax.axis_index("order"), lax.axis_index("chan")
    return order // 8, (order // 2) % 4, order % 2, chan // 4, chan % 4


def lanes(block):
    return pl.ds(pl.multiple_of(block * 128, 128), 128)


def kernel(
    rows, x_ref, g_ref, w_ref, back_ref, wgrad_ref,
    xz, gx, gp, gz, wt, acc, pair, part, relay, heap, fin, ret, wg,
    xa_s, xa_r, ga_s, ga_r, gi_s, gi_r, w_s, w_r, w_loc,
    xr_s, xl_s, xz_r, gr_s, gl_s, gz_r, gx_s, gx_r,
    pair_s, pair_r, wo_s, wo_r, far_s, far_r, rs_s, rs_r, rt_s, rt_r, out_s,
):
    zh, y, k, x, zl = coords()
    z = zh * 4 + zl
    half = rows // 2
    me = y * 2 + k

    def dev(zh_, y_, k_, x_, zl_):
        return (zh_ * 8 + y_ * 2 + k_, x_ * 4 + zl_)

    def at_z(z_):
        return dev(z_ // 4, y, k, x, z_ % 4)

    def greet(device):
        pl.semaphore_signal(pltpu.get_barrier_semaphore(), inc=1, device_id=device, device_id_type=MESH)

    def greet_order(t, _):
        other = (zh * 8 + me + t) % 16
        greet((other, x * 4 + zl))
        return 0

    lax.fori_loop(1, 16, greet_order, 0)
    for d in (1, 2, 3, 5, 6, 7):
        greet(at_z((z + d) % 8))
    for d in (1, 2, 3):
        for other in (0, 1):
            greet(dev(zh, y, other, (x + d) % 4, zl))
    pl.semaphore_wait(pltpu.get_barrier_semaphore(), 15 + 6 + 6)

    def remote(src, dst, send, recv, device):
        return pltpu.make_async_remote_copy(
            src_ref=src, dst_ref=dst, send_sem=send, recv_sem=recv, device_id=device, device_id_type=MESH
        )

    def blk(buf, b, lane):
        return buf.at[b, :, lanes(lane)]

    def to_weight(src, buf, lane, send, recv, t):
        e = (zh * 4 + y + t) % 8
        remote(src.at[e], blk(buf, me, lane), send.at[e], recv.at[me], dev(e // 4, e % 4, zh, x, zl)).start()

    def own_weight(src, buf, lane, recv, e):
        pltpu.make_async_copy(src.at[e], blk(buf, me, lane), recv.at[me]).start()

    def weight_out(src, buf, lane, send, recv):
        mine = zh == k

        @pl.when(mine)
        def _():
            own_weight(src, buf, lane, recv, zh * 4 + y)

        @pl.when(jnp.logical_not(mine))
        def _():
            to_weight(src, buf, lane, send, recv, 0)

        def step(t, _):
            to_weight(src, buf, lane, send, recv, t)
            return 0

        lax.fori_loop(1, 8, step, 0)

    def to_input(t):
        j = (me + t) % 8
        y_, k_ = j // 2, j % 2
        return remote(g_ref.at[4 * k_ + y_], blk(gz, me, zl), gi_s.at[j], gi_r.at[me], dev(zh, y_, k_, x, zl))

    def gi_step(t, _):
        to_input(t).start()
        return 0

    lax.fori_loop(1, 8, gi_step, 0)
    degree = 4 * k + y
    pltpu.make_async_copy(g_ref.at[degree], blk(gz, me, zl), gi_r.at[me]).start()
    weight_out(g_ref, gx, x, ga_s, ga_r)

    w_loc_copy = pltpu.make_async_copy(w_ref.at[:, degree, :, zl], wt.at[:, :, :, lanes(zl)], w_loc)
    w_loc_copy.start()
    w_copies = []
    for i, (d, part_of) in enumerate(((1, (0, 2)), (7, (0, 2)), (2, (0, 1)), (6, (1, 1)))):
        to = (z + d) % 8
        reim = pl.ds(*part_of)
        w_copies.append(
            remote(w_ref.at[reim, degree, :, to % 4], wt.at[reim, :, :, lanes(zl)], w_s.at[i], w_r.at[i], at_z(to))
        )
        w_copies[-1].start()

    def right(buf, o, b, send, recv):
        return remote(blk(buf, b, o), blk(buf, b, o), send.at[o, b], recv.at[o, b], dev(zh, y, k, x, (zl + 1) % 4))

    def left(buf, o, b, send, recv):
        return remote(blk(buf, b, o), blk(buf, b, o), send.at[o, b], recv.at[o, b], dev(zh, y, k, x, (zl + 3) % 4))

    def own_line(buf, b, s_r, s_l, recv):
        @pl.when(zl < 3)
        def _():
            right(buf, zl, b, s_r, recv).start()

        @pl.when(zl > 0)
        def _():
            left(buf, zl, b, s_l, recv).start()

    def pass_line(buf, b, d, s_r, s_l, recv):
        @pl.when(zl >= d)
        def _():
            o = zl - d
            right(buf, o, b, s_r, recv).wait_recv()

            @pl.when(zl < 3)
            def _():
                right(buf, o, b, s_r, recv).start()

        @pl.when(zl + d <= 3)
        def _():
            o = zl + d
            left(buf, o, b, s_l, recv).wait_recv()

            @pl.when(zl > 0)
            def _():
                left(buf, o, b, s_l, recv).start()

    def drain_line(buf, b, s_r, s_l, recv):
        for d in range(3):
            @pl.when((zl >= d) & (zl < 3))
            def _():
                right(buf, zl - d, b, s_r, recv).wait_send()

            @pl.when((zl + d <= 3) & (zl > 0))
            def _():
                left(buf, zl + d, b, s_l, recv).wait_send()

    def ring_right(o, b):
        return remote(blk(gx, b, o), blk(gx, b, o), gx_s.at[0, b], gx_r.at[0, b], dev(zh, y, k, (x + 1) % 4, zl))

    def ring_left(o, b):
        return remote(blk(gx, b, o), blk(gx, b, o), gx_s.at[1, b], gx_r.at[1, b], dev(zh, y, k, (x + 3) % 4, zl))

    def ring_far(to_right, b):
        o, to = ((x + 3) % 4, (x + 1) % 4) if to_right else ((x + 1) % 4, (x + 3) % 4)
        return remote(blk(gx, b, o), blk(gx, b, o), gx_s.at[2, b], gx_r.at[2, b], dev(zh, y, k, to, zl))

    def pair_of(c):
        return (2 * c, 2 * c + 1)

    def g_own(c):
        for b in pair_of(c):
            pltpu.make_async_copy(g_ref.at[0], blk(gz, b, zl), gi_r.at[b]).wait()
            own_line(gz, b, gr_s, gl_s, gz_r)

    def g_pass(c, d):
        for b in pair_of(c):
            pass_line(gz, b, d, gr_s, gl_s, gz_r)

    def x_own(c):
        for b in pair_of(c):
            pltpu.make_async_copy(x_ref.at[0], blk(xz, b, zl), xa_r.at[b]).wait()
            own_line(xz, b, xr_s, xl_s, xz_r)

    def x_pass(c, d):
        for b in pair_of(c):
            pass_line(xz, b, d, xr_s, xl_s, xz_r)

    def ring_own(c):
        for b in pair_of(c):
            pltpu.make_async_copy(g_ref.at[0], blk(gx, b, x), ga_r.at[b]).wait()
            ring_right(x, b).start()
            ring_left(x, b).start()

    def ring_pass(c):
        even, odd = pair_of(c)
        for b in (even, odd):
            ring_right((x + 3) % 4, b).wait_recv()
            ring_left((x + 1) % 4, b).wait_recv()
        ring_far(True, even).start()
        ring_far(False, odd).start()

    def ring_end(c):
        even, odd = pair_of(c)
        ring_far(True, even).wait_recv()
        ring_far(False, odd).wait_recv()
        cot = gx[pl.ds(2 * c, 2)]
        gp[pl.ds(2 * c, 2), 0:half] = cot[:, half:]
        gp[pl.ds(2 * c, 2), half:rows] = -cot[:, :half]

    def far(way, c):
        x_ = (x + 2) % 4
        at = pl.ds(0, half) if way == 0 else pl.ds(half, half)
        return remote(
            part.at[x_, pl.ds(2 * c, 2), at], relay.at[way, pl.ds(2 * c, 2)], far_s.at[way, c], far_r.at[way, c],
            dev(zh, y, k, (x + 1 + 2 * way) % 4, zl),
        )

    def near(way, c):
        x_ = (x + 1 + 2 * way) % 4
        return remote(
            part.at[x_, pl.ds(2 * c, 2)], heap.at[way, pl.ds(2 * c, 2)], rs_s.at[way, c], rs_r.at[way, c],
            dev(zh, y, k, x_, zl),
        )

    def back_relay(c):
        for way in (0, 1):
            far(way, c).wait_recv()
            x_ = (x + 1 + 2 * way) % 4
            for b in pair_of(c):
                if way == 0:
                    part[x_, b, 0:half] = part[x_, b, 0:half] + relay[way, b]
                else:
                    part[x_, b, half:rows] = part[x_, b, half:rows] + relay[way, b]
            near(way, c).start()

    def home(b):
        y_, k_ = b // 2, b % 2
        return remote(fin.at[b], ret.at[degree], rt_s.at[b], rt_r.at[degree], dev(zh, y_, k_, x, zl))

    def back_reduce(c):
        for way in (0, 1):
            near(way, c).wait_recv()
        for b in pair_of(c):
            fin[b] = part[x, b] + (heap[0, b] + heap[1, b])

            @pl.when(b == me)
            def _():
                pltpu.make_async_copy(fin.at[b], ret.at[degree], rt_r.at[degree]).start()

            @pl.when(b != me)
            def _():
                home(b).start()

    def back_product(c):
        cot = gz[pl.ds(2 * c, 2)].reshape(2 * rows, 512)
        over_lanes = (((1,), (1,)), ((), ()))
        by_re = lax.dot_general(cot, wt[0].reshape(512, 512), over_lanes, preferred_element_type=F32)
        by_im = lax.dot_general(cot, wt[1].reshape(512, 512), over_lanes, preferred_element_type=F32)
        for j in range(2):
            lo, mid, hi = j * rows, j * rows + half, (j + 1) * rows
            back_re = by_re[lo:mid] + by_im[mid:hi]
            back_im = by_re[mid:hi] - by_im[lo:mid]
            for x_ in range(NX):
                part[x_, 2 * c + j, 0:half] = back_re[:, x_ * 128 : (x_ + 1) * 128]
                part[x_, 2 * c + j, half:rows] = back_im[:, x_ * 128 : (x_ + 1) * 128]
        for way in (0, 1):
            far(way, c).start()

    def when_chunk(c, work):
        @pl.when((c >= 0) & (c < 4))
        def _():
            work(c)

    def pipeline(s, _):
        when_chunk(s, g_own)
        when_chunk(s - 1, lambda c: g_pass(c, 1))
        when_chunk(s - 1, ring_own)
        when_chunk(s - 2, lambda c: g_pass(c, 2))

        @pl.when(s == 3)
        def _():
            weight_out(x_ref, xz, zl, xa_s, xa_r)
            w_loc_copy.wait()
            for copy in w_copies:
                copy.wait_recv()

        def product(c):
            g_pass(c, 3)
            back_product(c)

        when_chunk(s - 3, product)
        when_chunk(s - 2, ring_pass)
        when_chunk(s - 4, back_relay)
        when_chunk(s - 5, x_own)
        when_chunk(s - 5, back_reduce)
        when_chunk(s - 6, lambda c: x_pass(c, 1))
        when_chunk(s - 6, ring_end)
        when_chunk(s - 7, lambda c: x_pass(c, 2))
        return 0

    lax.fori_loop(0, 11, pipeline, 0)

    order_of = jnp.where(zl == 0, 0o3210, jnp.where(zl == 1, 0o3201, jnp.where(zl == 2, 0o0312, 0o0123)))

    def nth(t):
        return (order_of // jnp.where(t == 0, 1, jnp.where(t == 1, 8, jnp.where(t == 2, 64, 512)))) % 8

    def swap(o):
        return remote(acc.at[1 - k, o], pair.at[o], pair_s.at[o], pair_r.at[o], dev(zh, y, 1 - k, x, zl))

    def owner_rows(o):
        return pl.ds(pl.multiple_of((x % 2) * 512 + o * 128, 128), 128)

    def wgrad_to(d, o):
        return remote(
            acc.at[k, o, :, lanes((x + d) % 4)], wg.at[k, owner_rows(o)],
            wo_s.at[d, o], wo_r.at[x % 2, k, o], dev(zh, y, x // 2, (x + d) % 4, zl),
        )

    def wgrad_product(t):
        o = nth(t)

        @pl.when(t == 3)
        def _():
            def last(b, _):
                pass_line(xz, b, 3, xr_s, xl_s, xz_r)
                return 0

            lax.fori_loop(0, NB, last, 0)

        left_ = xz[:, :, lanes(o)].reshape(NB * rows, 128)
        over_rows = (((0,), (0,)), ((), ()))
        acc[0, o] = lax.dot_general(left_, gx[...].reshape(NB * rows, 512), over_rows, preferred_element_type=F32)
        acc[1, o] = lax.dot_general(left_, gp[...].reshape(NB * rows, 512), over_rows, preferred_element_type=F32)
        swap(o).start()

    def wgrad_send(t):
        o = nth(t)
        swap(o).wait_recv()
        acc[k, o] = acc[k, o] + pair[o]
        for d in (1, 3, 2):
            wgrad_to(d, o).start()

        @pl.when(k == x // 2)
        def _():
            pltpu.make_async_copy(
                acc.at[k, o, :, lanes(x)], wg.at[k, owner_rows(o)], wo_r.at[x % 2, k, o]
            ).start()

        @pl.when(k != x // 2)
        def _():
            wgrad_to(0, o).start()

    def wgrad_step(t, _):
        @pl.when(t < 4)
        def _():
            wgrad_product(t)

        @pl.when(t > 0)
        def _():
            wgrad_send(t - 1)

        return 0

    lax.fori_loop(0, 5, wgrad_step, 0)

    def returned(l, _):
        pltpu.make_async_copy(fin.at[0], ret.at[l], rt_r.at[l]).wait()
        return 0

    lax.fori_loop(0, NB, returned, 0)
    back_out = pltpu.make_async_copy(ret, back_ref, out_s.at[1])
    back_out.start()

    def owned(o, _):
        for r in range(2):
            for k_ in range(2):
                at = pl.ds(pl.multiple_of(r * 512 + o * 128, 128), 128)
                pltpu.make_async_copy(acc.at[0, 0, :, pl.ds(0, 128)], wg.at[k_, at], wo_r.at[r, k_, o]).wait()
        return 0

    lax.fori_loop(0, NZ, owned, 0)
    wg_out = pltpu.make_async_copy(wg, wgrad_ref, out_s.at[0])
    wg_out.start()

    def drain(b, _):
        drain_line(xz, b, xr_s, xl_s, xz_r)
        drain_line(gz, b, gr_s, gl_s, gz_r)
        for send in (0, 1, 2):
            remote(blk(gx, b, x), blk(gx, b, x), gx_s.at[send, b], gx_r.at[0, b], dev(zh, y, 1 - k, x, zl)).wait_send()

        @pl.when(jnp.logical_or(zh != k, b != zh * 4 + y))
        def _():
            pltpu.make_async_copy(x_ref.at[b], blk(xz, 0, zl), xa_s.at[b]).wait()
            pltpu.make_async_copy(g_ref.at[b], blk(gx, 0, x), ga_s.at[b]).wait()

        @pl.when(b != me)
        def _():
            pltpu.make_async_copy(g_ref.at[0], blk(gz, 0, zl), gi_s.at[b]).wait()
            home(b).wait_send()

        return 0

    lax.fori_loop(0, NB, drain, 0)

    def drain_scatter(c, _):
        for way in (0, 1):
            far(way, c).wait_send()
            near(way, c).wait_send()
        return 0

    lax.fori_loop(0, NB // 2, drain_scatter, 0)
    for copy in w_copies:
        copy.wait_send()

    def drain_wgrad(o, _):
        swap(o).wait_send()
        for d in (1, 2, 3):
            wgrad_to(d, o).wait_send()

        @pl.when(k != x // 2)
        def _():
            wgrad_to(0, o).wait_send()

        return 0

    lax.fori_loop(0, NZ, drain_wgrad, 0)

    wg_out.wait()
    back_out.wait()


def per_device(window, inputs, out_grad, weights):
    _, samples, degrees, orders, width = inputs.shape
    first_order = lax.axis_index("order") * orders
    degree = window[0] + jnp.arange(degrees, dtype=jnp.int32)
    order = first_order + jnp.arange(orders, dtype=jnp.int32)
    live = (order[None, :] <= degree[:, None]).astype(BF16)[:, :, None]
    real = samples * orders
    half = -(-real // 16) * 16
    rows = 2 * half

    def by_degree(a):
        a = (a * live).transpose(2, 0, 1, 3, 4).reshape(degrees, 2, real, width)
        return jnp.pad(a, ((0, 0), (0, 0), (0, half - real), (0, 0))).reshape(degrees, rows, width)

    dma, vmem = pltpu.SemaphoreType.DMA, pltpu.VMEM
    back, wgrad = pl.pallas_call(
        functools.partial(kernel, rows),
        name="mix_back",
        out_shape=(
            jax.ShapeDtypeStruct((degrees, rows, width), F32),
            jax.ShapeDtypeStruct((2, 1024, width), F32),
        ),
        in_specs=[
            pl.BlockSpec(memory_space=pltpu.VMEM),
            pl.BlockSpec(memory_space=pltpu.VMEM),
            pl.BlockSpec(memory_space=pl.ANY),
        ],
        out_specs=(pl.BlockSpec(memory_space=pl.ANY), pl.BlockSpec(memory_space=pl.ANY)),
        scratch_shapes=[
            vmem((NB, rows, 512), BF16),
            vmem((NB, rows, 512), BF16),
            vmem((NB, rows, 512), BF16),
            vmem((NB, rows, 512), BF16),
            vmem((2, 4, 128, 512), BF16),
            vmem((2, NZ, 128, 512), F32),
            vmem((NZ, 128, 512), F32),
            vmem((NX, NB, rows, 128), F32),
            vmem((2, NB, half, 128), F32),
            vmem((2, NB, rows, 128), F32),
            vmem((NB, rows, 128), F32),
            vmem((NB, rows, 128), F32),
            vmem((2, 1024, 128), F32),
            dma((8,)), dma((8,)), dma((8,)), dma((8,)), dma((8,)), dma((8,)), dma((4,)), dma((4,)), dma(()),
            dma((4, 8)), dma((4, 8)), dma((4, 8)), dma((4, 8)), dma((4, 8)), dma((4, 8)), dma((3, 8)), dma((3, 8)),
            dma((4,)), dma((4,)), dma((4, 4)), dma((2, 2, 4)), dma((2, 4)), dma((2, 4)), dma((2, 4)), dma((2, 4)), dma((8,)), dma((8,)), dma((2,)),
        ],
        compiler_params=pltpu.CompilerParams(
            collective_id=0, has_side_effects=True, vmem_limit_bytes=44 * 2**20
        ),
    )(by_degree(inputs), by_degree(out_grad), weights.reshape(2, degrees, 4, 4, 128, width))
    back = back.reshape(degrees, 2, half, width)[:, :, :real].reshape(degrees, 2, samples, orders, width)
    return back.transpose(1, 2, 0, 3, 4), wgrad


def solution(mesh):
    placed = (
        P(),
        P(None, None, None, "order", "chan"),
        P(None, None, None, "order", "chan"),
        P(None, None, "chan"),
    )
    return jax.shard_map(
        per_device,
        mesh=mesh,
        in_specs=placed,
        out_specs=(P(None, None, None, "order", "chan"), P(None, "order", "chan")),
        check_vma=False,
    )
```

```python
import functools

import jax
import jax.numpy as jnp
from jax import lax
from jax.experimental import pallas as pl
from jax.experimental.pallas import tpu as pltpu
from jax.sharding import PartitionSpec as P

MESH = pl.DeviceIdType.MESH
BF16, F32 = jnp.bfloat16, jnp.float32

NX, NY, NZ = 4, 4, 4
NB = 8


def coords():
    order, chan = lax.axis_index("order"), lax.axis_index("chan")
    return order // 8, (order // 2) % 4, order % 2, chan // 4, chan % 4


def lanes(block):
    return pl.ds(pl.multiple_of(block * 128, 128), 128)


def kernel(
    rows, x_ref, g_ref, w_ref, back_ref, wgrad_ref,
    xz, xc, xt, gx, gp, gz, wt, acc, pair, part, relay, heap, fin, ret, wg,
    xa_s, xa_r, xc_r, xc_s, xt_r, ga_s, ga_r, gi_s, gi_r, w_s, w_r, w_loc,
    xr_s, xl_s, xz_r, gr_s, gl_s, gz_r, gx_s, gx_r,
    pair_s, pair_r, wo_s, wo_r, far_s, far_r, rs_s, rs_r, rt_s, rt_r, out_s,
):
    zh, y, k, x, zl = coords()
    z = zh * 4 + zl
    half = rows // 2
    me = y * 2 + k

    def dev(zh_, y_, k_, x_, zl_):
        return (zh_ * 8 + y_ * 2 + k_, x_ * 4 + zl_)

    def at_z(z_):
        return dev(z_ // 4, y, k, x, z_ % 4)

    def greet(device):
        pl.semaphore_signal(pltpu.get_barrier_semaphore(), inc=1, device_id=device, device_id_type=MESH)

    def greet_order(t, _):
        other = (zh * 8 + me + t) % 16
        greet((other, x * 4 + zl))
        return 0

    lax.fori_loop(1, 16, greet_order, 0)
    for d in (1, 2, 3, 5, 6, 7):
        greet(at_z((z + d) % 8))
    for d in (1, 2, 3):
        for other in (0, 1):
            greet(dev(zh, y, other, (x + d) % 4, zl))
    pl.semaphore_wait(pltpu.get_barrier_semaphore(), 15 + 6 + 6)

    def remote(src, dst, send, recv, device):
        return pltpu.make_async_remote_copy(
            src_ref=src, dst_ref=dst, send_sem=send, recv_sem=recv, device_id=device, device_id_type=MESH
        )

    def blk(buf, b, lane):
        return buf.at[b, :, lanes(lane)]

    def to_weight(src, buf, lane, send, recv, t):
        e = (zh * 4 + y + t) % 8
        remote(src.at[e], blk(buf, me, lane), send.at[e], recv.at[me], dev(e // 4, e % 4, zh, x, zl)).start()

    def own_weight(src, buf, lane, recv, e):
        pltpu.make_async_copy(src.at[e], blk(buf, me, lane), recv.at[me]).start()

    def weight_out(src, buf, lane, send, recv):
        mine = zh == k

        @pl.when(mine)
        def _():
            own_weight(src, buf, lane, recv, zh * 4 + y)

        @pl.when(jnp.logical_not(mine))
        def _():
            to_weight(src, buf, lane, send, recv, 0)

        def step(t, _):
            to_weight(src, buf, lane, send, recv, t)
            return 0

        lax.fori_loop(1, 8, step, 0)

    def to_input(t):
        j = (me + t) % 8
        y_, k_ = j // 2, j % 2
        return remote(g_ref.at[4 * k_ + y_], blk(gz, me, zl), gi_s.at[j], gi_r.at[me], dev(zh, y_, k_, x, zl))

    def gi_step(t, _):
        to_input(t).start()
        return 0

    lax.fori_loop(1, 8, gi_step, 0)
    degree = 4 * k + y
    pltpu.make_async_copy(g_ref.at[degree], blk(gz, me, zl), gi_r.at[me]).start()
    weight_out(g_ref, gx, x, ga_s, ga_r)

    source = zh == k

    def x_out(t, _):
        y_ = (y + t) % 4
        mine, other = zh * 4 + y_, (1 - zh) * 4 + y_
        itself = jnp.logical_and(source, t == 0)

        @pl.when(itself)
        def _():
            pltpu.make_async_copy(x_ref.at[mine], blk(xz, me, zl), xa_r.at[me]).start()
            pltpu.make_async_copy(x_ref.at[other], xc.at[me], xc_r.at[me]).start()

        @pl.when(jnp.logical_not(itself))
        def _():
            to = dev(zh, y_, zh, x, zl)
            remote(x_ref.at[mine], blk(xz, me, zl), xa_s.at[mine], xa_r.at[me], to).start()
            remote(x_ref.at[other], xc.at[me], xa_s.at[other], xc_r.at[me], to).start()

        return 0

    lax.fori_loop(0, 4, x_out, 0)

    w_loc_copy = pltpu.make_async_copy(w_ref.at[:, degree, :, zl], wt.at[:, :, :, lanes(zl)], w_loc)
    w_loc_copy.start()
    w_copies = []
    for i, (d, part_of) in enumerate(((1, (0, 2)), (7, (0, 2)), (2, (0, 1)), (6, (1, 1)))):
        to = (z + d) % 8
        reim = pl.ds(*part_of)
        w_copies.append(
            remote(w_ref.at[reim, degree, :, to % 4], wt.at[reim, :, :, lanes(zl)], w_s.at[i], w_r.at[i], at_z(to))
        )
        w_copies[-1].start()

    def right(buf, o, b, send, recv):
        return remote(blk(buf, b, o), blk(buf, b, o), send.at[o, b], recv.at[o, b], dev(zh, y, k, x, (zl + 1) % 4))

    def left(buf, o, b, send, recv):
        return remote(blk(buf, b, o), blk(buf, b, o), send.at[o, b], recv.at[o, b], dev(zh, y, k, x, (zl + 3) % 4))

    def own_line(buf, b, s_r, s_l, recv):
        @pl.when(zl < 3)
        def _():
            right(buf, zl, b, s_r, recv).start()

        @pl.when(zl > 0)
        def _():
            left(buf, zl, b, s_l, recv).start()

    def pass_line(buf, b, d, s_r, s_l, recv):
        @pl.when(zl >= d)
        def _():
            o = zl - d
            right(buf, o, b, s_r, recv).wait_recv()

            @pl.when(zl < 3)
            def _():
                right(buf, o, b, s_r, recv).start()

        @pl.when(zl + d <= 3)
        def _():
            o = zl + d
            left(buf, o, b, s_l, recv).wait_recv()

            @pl.when(zl > 0)
            def _():
                left(buf, o, b, s_l, recv).start()

    def drain_line(buf, b, s_r, s_l, recv):
        for d in range(3):
            @pl.when((zl >= d) & (zl < 3))
            def _():
                right(buf, zl - d, b, s_r, recv).wait_send()

            @pl.when((zl + d <= 3) & (zl > 0))
            def _():
                left(buf, zl + d, b, s_l, recv).wait_send()

    def ring_right(o, b):
        return remote(blk(gx, b, o), blk(gx, b, o), gx_s.at[0, b], gx_r.at[0, b], dev(zh, y, k, (x + 1) % 4, zl))

    def ring_left(o, b):
        return remote(blk(gx, b, o), blk(gx, b, o), gx_s.at[1, b], gx_r.at[1, b], dev(zh, y, k, (x + 3) % 4, zl))

    def ring_far(to_right, b):
        o, to = ((x + 3) % 4, (x + 1) % 4) if to_right else ((x + 1) % 4, (x + 3) % 4)
        return remote(blk(gx, b, o), blk(gx, b, o), gx_s.at[2, b], gx_r.at[2, b], dev(zh, y, k, to, zl))

    def pair_of(c):
        return (2 * c, 2 * c + 1)

    def g_own(c):
        for b in pair_of(c):
            pltpu.make_async_copy(g_ref.at[0], blk(gz, b, zl), gi_r.at[b]).wait()
            own_line(gz, b, gr_s, gl_s, gz_r)

    def g_pass(c, d):
        for b in pair_of(c):
            pass_line(gz, b, d, gr_s, gl_s, gz_r)

    def x_right(src, o, b, send):
        return remote(src, blk(xz, b, o), send, xz_r.at[o, b], at_z((z + 1) % 8))

    def x_left(src, o, b, send):
        return remote(src, blk(xz, b, o), send, xz_r.at[o, b], at_z((z + 7) % 8))

    def transit(b, d):
        return remote(xc.at[b], xt.at[b], xc_s.at[0, b], xt_r.at[b], at_z((z + d) % 8))

    def x_cross(b):
        @pl.when(zl == 3)
        def _():
            x_right(xc.at[b], 3, b, xc_s.at[0, b]).start()

        @pl.when(zl == 0)
        def _():
            x_left(xc.at[b], 0, b, xc_s.at[0, b]).start()

        @pl.when(zl == 2)
        def _():
            transit(b, 1).start()

        @pl.when(zl == 1)
        def _():
            transit(b, 7).start()

    def x_transit(b):
        @pl.when(zl == 3)
        def _():
            transit(b, 1).wait_recv()
            x_right(xt.at[b], 2, b, xc_s.at[1, b]).start()

        @pl.when(zl == 0)
        def _():
            transit(b, 7).wait_recv()
            x_left(xt.at[b], 1, b, xc_s.at[1, b]).start()

    def x_own(c):
        @pl.when(source)
        def _():
            for b in pair_of(c):
                pltpu.make_async_copy(x_ref.at[0], xc.at[b], xc_r.at[b]).wait()
                x_cross(b)
                pltpu.make_async_copy(x_ref.at[0], blk(xz, b, zl), xa_r.at[b]).wait()
                own_line(xz, b, xr_s, xl_s, xz_r)

    def x_arrive(b, o, to_right):
        if to_right:
            x_right(blk(xz, b, o), o, b, xr_s.at[o, b]).wait_recv()

            @pl.when(zl < 3)
            def _():
                x_right(blk(xz, b, o), o, b, xr_s.at[o, b]).start()
        else:
            x_left(blk(xz, b, o), o, b, xl_s.at[o, b]).wait_recv()

            @pl.when(zl > 0)
            def _():
                x_left(blk(xz, b, o), o, b, xl_s.at[o, b]).start()

    def x_hop(c, hops):
        @pl.when(source)
        def _():
            for b in pair_of(c):
                if hops == 1:
                    x_transit(b)
                if hops <= 3:
                    pass_line(xz, b, hops, xr_s, xl_s, xz_r)

        @pl.when(jnp.logical_not(source))
        def _():
            for b in pair_of(c):
                for o, first in ((3, zl + 1), (2, zl + 2), (0, 4 - zl), (1, 5 - zl)):
                    @pl.when(first == hops)
                    def _():
                        x_arrive(b, o, o >= 2)

    def ring_own(c):
        for b in pair_of(c):
            pltpu.make_async_copy(g_ref.at[0], blk(gx, b, x), ga_r.at[b]).wait()
            ring_right(x, b).start()
            ring_left(x, b).start()

    def ring_pass(c):
        even, odd = pair_of(c)
        for b in (even, odd):
            ring_right((x + 3) % 4, b).wait_recv()
            ring_left((x + 1) % 4, b).wait_recv()
        ring_far(True, even).start()
        ring_far(False, odd).start()

    def ring_end(c):
        even, odd = pair_of(c)
        ring_far(True, even).wait_recv()
        ring_far(False, odd).wait_recv()
        cot = gx[pl.ds(2 * c, 2)]
        gp[pl.ds(2 * c, 2), 0:half] = cot[:, half:]
        gp[pl.ds(2 * c, 2), half:rows] = -cot[:, :half]

    def far(way, c):
        x_ = (x + 2) % 4
        at = pl.ds(0, half) if way == 0 else pl.ds(half, half)
        return remote(
            part.at[x_, pl.ds(2 * c, 2), at], relay.at[way, pl.ds(2 * c, 2)], far_s.at[way, c], far_r.at[way, c],
            dev(zh, y, k, (x + 1 + 2 * way) % 4, zl),
        )

    def near(way, c):
        x_ = (x + 1 + 2 * way) % 4
        return remote(
            part.at[x_, pl.ds(2 * c, 2)], heap.at[way, pl.ds(2 * c, 2)], rs_s.at[way, c], rs_r.at[way, c],
            dev(zh, y, k, x_, zl),
        )

    def back_relay(c):
        for way in (0, 1):
            far(way, c).wait_recv()
            x_ = (x + 1 + 2 * way) % 4
            for b in pair_of(c):
                if way == 0:
                    part[x_, b, 0:half] = part[x_, b, 0:half] + relay[way, b]
                else:
                    part[x_, b, half:rows] = part[x_, b, half:rows] + relay[way, b]
            near(way, c).start()

    def home(b):
        y_, k_ = b // 2, b % 2
        return remote(fin.at[b], ret.at[degree], rt_s.at[b], rt_r.at[degree], dev(zh, y_, k_, x, zl))

    def back_reduce(c):
        for way in (0, 1):
            near(way, c).wait_recv()
        for b in pair_of(c):
            fin[b] = part[x, b] + (heap[0, b] + heap[1, b])

            @pl.when(b == me)
            def _():
                pltpu.make_async_copy(fin.at[b], ret.at[degree], rt_r.at[degree]).start()

            @pl.when(b != me)
            def _():
                home(b).start()

    def back_product(c):
        cot = gz[pl.ds(2 * c, 2)].reshape(2 * rows, 512)
        over_lanes = (((1,), (1,)), ((), ()))
        by_re = lax.dot_general(cot, wt[0].reshape(512, 512), over_lanes, preferred_element_type=F32)
        by_im = lax.dot_general(cot, wt[1].reshape(512, 512), over_lanes, preferred_element_type=F32)
        for j in range(2):
            lo, mid, hi = j * rows, j * rows + half, (j + 1) * rows
            back_re = by_re[lo:mid] + by_im[mid:hi]
            back_im = by_re[mid:hi] - by_im[lo:mid]
            for x_ in range(NX):
                part[x_, 2 * c + j, 0:half] = back_re[:, x_ * 128 : (x_ + 1) * 128]
                part[x_, 2 * c + j, half:rows] = back_im[:, x_ * 128 : (x_ + 1) * 128]
        for way in (0, 1):
            far(way, c).start()

    def nth(t):
        o = 3 - t if t < 2 else t - 2
        return jnp.where(zl < 2, o, 3 - o)

    def swap(o):
        return remote(acc.at[1 - k, o], pair.at[o], pair_s.at[o], pair_r.at[o], dev(zh, y, 1 - k, x, zl))

    def owner_rows(o):
        return pl.ds(pl.multiple_of((x % 2) * 512 + o * 128, 128), 128)

    def wgrad_to(d, o):
        return remote(
            acc.at[k, o, :, lanes((x + d) % 4)], wg.at[k, owner_rows(o)],
            wo_s.at[d, o], wo_r.at[x % 2, k, o], dev(zh, y, x // 2, (x + d) % 4, zl),
        )

    def wgrad_product(t):
        o = nth(t)

        left_ = xz[:, :, lanes(o)].reshape(NB * rows, 128)
        over_rows = (((0,), (0,)), ((), ()))
        acc[0, o] = lax.dot_general(left_, gx[...].reshape(NB * rows, 512), over_rows, preferred_element_type=F32)
        acc[1, o] = lax.dot_general(left_, gp[...].reshape(NB * rows, 512), over_rows, preferred_element_type=F32)
        swap(o).start()

    def wgrad_send(t):
        o = nth(t)
        swap(o).wait_recv()
        acc[k, o] = acc[k, o] + pair[o]
        for d in (1, 3, 2):
            wgrad_to(d, o).start()

        @pl.when(k == x // 2)
        def _():
            pltpu.make_async_copy(
                acc.at[k, o, :, lanes(x)], wg.at[k, owner_rows(o)], wo_r.at[x % 2, k, o]
            ).start()

        @pl.when(k != x // 2)
        def _():
            wgrad_to(0, o).start()

    def when_chunk(c, work):
        @pl.when((c >= 0) & (c < 4))
        def _():
            work(c)

    def pipeline(s, _):
        when_chunk(s, g_own)
        when_chunk(s - 1, lambda c: g_pass(c, 1))
        when_chunk(s - 1, ring_own)
        when_chunk(s - 2, lambda c: g_pass(c, 2))

        @pl.when(s == 3)
        def _():
            w_loc_copy.wait()
            for copy in w_copies:
                copy.wait_recv()

        def product(c):
            g_pass(c, 3)
            back_product(c)

        when_chunk(s - 3, product)
        when_chunk(s - 2, ring_pass)
        when_chunk(s - 3, x_own)
        when_chunk(s - 4, back_relay)
        when_chunk(s - 4, lambda c: x_hop(c, 1))
        when_chunk(s - 5, back_reduce)
        when_chunk(s - 5, lambda c: x_hop(c, 2))
        when_chunk(s - 5, ring_end)
        when_chunk(s - 6, lambda c: x_hop(c, 3))
        when_chunk(s - 7, lambda c: x_hop(c, 4))

        @pl.when(s == 10)
        def _():
            wgrad_product(0)
            wgrad_product(1)

        @pl.when(s == 11)
        def _():
            wgrad_send(0)
            wgrad_product(2)
            wgrad_send(1)

        when_chunk(s - 8, lambda c: x_hop(c, 5))
        return 0

    lax.fori_loop(0, 12, pipeline, 0)
    wgrad_product(3)
    wgrad_send(2)
    wgrad_send(3)

    def returned(l, _):
        pltpu.make_async_copy(fin.at[0], ret.at[l], rt_r.at[l]).wait()
        return 0

    lax.fori_loop(0, NB, returned, 0)
    back_out = pltpu.make_async_copy(ret, back_ref, out_s.at[1])
    back_out.start()

    def owned(o, _):
        for r in range(2):
            for k_ in range(2):
                at = pl.ds(pl.multiple_of(r * 512 + o * 128, 128), 128)
                pltpu.make_async_copy(acc.at[0, 0, :, pl.ds(0, 128)], wg.at[k_, at], wo_r.at[r, k_, o]).wait()
        return 0

    lax.fori_loop(0, NZ, owned, 0)
    wg_out = pltpu.make_async_copy(wg, wgrad_ref, out_s.at[0])
    wg_out.start()

    def drain(b, _):
        @pl.when(source)
        def _():
            drain_line(xz, b, xr_s, xl_s, xz_r)
            x_right(xc.at[b], 3, b, xc_s.at[0, b]).wait_send()

            @pl.when((zl == 0) | (zl == 3))
            def _():
                x_right(xt.at[b], 2, b, xc_s.at[1, b]).wait_send()

        @pl.when(jnp.logical_not(source))
        def _():
            for o in (0, 1, 2, 3):
                if o >= 2:
                    @pl.when(zl < 3)
                    def _():
                        x_right(blk(xz, b, o), o, b, xr_s.at[o, b]).wait_send()
                else:
                    @pl.when(zl > 0)
                    def _():
                        x_left(blk(xz, b, o), o, b, xl_s.at[o, b]).wait_send()

        drain_line(gz, b, gr_s, gl_s, gz_r)
        for send in (0, 1, 2):
            remote(blk(gx, b, x), blk(gx, b, x), gx_s.at[send, b], gx_r.at[0, b], dev(zh, y, 1 - k, x, zl)).wait_send()

        @pl.when(jnp.logical_or(zh != k, b != zh * 4 + y))
        def _():
            pltpu.make_async_copy(g_ref.at[b], blk(gx, 0, x), ga_s.at[b]).wait()

        @pl.when(jnp.logical_or(zh != k, b % 4 != y))
        def _():
            pltpu.make_async_copy(x_ref.at[b], blk(xz, 0, zl), xa_s.at[b]).wait()

        @pl.when(b != me)
        def _():
            pltpu.make_async_copy(g_ref.at[0], blk(gz, 0, zl), gi_s.at[b]).wait()
            home(b).wait_send()

        return 0

    lax.fori_loop(0, NB, drain, 0)

    def drain_scatter(c, _):
        for way in (0, 1):
            far(way, c).wait_send()
            near(way, c).wait_send()
        return 0

    lax.fori_loop(0, NB // 2, drain_scatter, 0)
    for copy in w_copies:
        copy.wait_send()

    def drain_wgrad(o, _):
        swap(o).wait_send()
        for d in (1, 2, 3):
            wgrad_to(d, o).wait_send()

        @pl.when(k != x // 2)
        def _():
            wgrad_to(0, o).wait_send()

        return 0

    lax.fori_loop(0, NZ, drain_wgrad, 0)

    wg_out.wait()
    back_out.wait()


def per_device(window, inputs, out_grad, weights):
    _, samples, degrees, orders, width = inputs.shape
    first_order = lax.axis_index("order") * orders
    degree = window[0] + jnp.arange(degrees, dtype=jnp.int32)
    order = first_order + jnp.arange(orders, dtype=jnp.int32)
    live = (order[None, :] <= degree[:, None]).astype(BF16)[:, :, None]
    real = samples * orders
    half = -(-real // 16) * 16
    rows = 2 * half

    def by_degree(a):
        a = (a * live).transpose(2, 0, 1, 3, 4).reshape(degrees, 2, real, width)
        return jnp.pad(a, ((0, 0), (0, 0), (0, half - real), (0, 0))).reshape(degrees, rows, width)

    dma, vmem = pltpu.SemaphoreType.DMA, pltpu.VMEM
    back, wgrad = pl.pallas_call(
        functools.partial(kernel, rows),
        name="mix_back",
        out_shape=(
            jax.ShapeDtypeStruct((degrees, rows, width), F32),
            jax.ShapeDtypeStruct((2, 1024, width), F32),
        ),
        in_specs=[
            pl.BlockSpec(memory_space=pltpu.VMEM),
            pl.BlockSpec(memory_space=pltpu.VMEM),
            pl.BlockSpec(memory_space=pl.ANY),
        ],
        out_specs=(pl.BlockSpec(memory_space=pl.ANY), pl.BlockSpec(memory_space=pl.ANY)),
        scratch_shapes=[
            vmem((NB, rows, 512), BF16),
            vmem((NB, rows, 128), BF16),
            vmem((NB, rows, 128), BF16),
            vmem((NB, rows, 512), BF16),
            vmem((NB, rows, 512), BF16),
            vmem((NB, rows, 512), BF16),
            vmem((2, 4, 128, 512), BF16),
            vmem((2, NZ, 128, 512), F32),
            vmem((NZ, 128, 512), F32),
            vmem((NX, NB, rows, 128), F32),
            vmem((2, NB, half, 128), F32),
            vmem((2, NB, rows, 128), F32),
            vmem((NB, rows, 128), F32),
            vmem((NB, rows, 128), F32),
            vmem((2, 1024, 128), F32),
            dma((8,)), dma((8,)), dma((8,)), dma((2, 8)), dma((8,)),
            dma((8,)), dma((8,)), dma((8,)), dma((8,)), dma((4,)), dma((4,)), dma(()),
            dma((4, 8)), dma((4, 8)), dma((4, 8)), dma((4, 8)), dma((4, 8)), dma((4, 8)), dma((3, 8)), dma((3, 8)),
            dma((4,)), dma((4,)), dma((4, 4)), dma((2, 2, 4)), dma((2, 4)), dma((2, 4)), dma((2, 4)), dma((2, 4)), dma((8,)), dma((8,)), dma((2,)),
        ],
        compiler_params=pltpu.CompilerParams(
            collective_id=0, has_side_effects=True, vmem_limit_bytes=44 * 2**20
        ),
    )(by_degree(inputs), by_degree(out_grad), weights.reshape(2, degrees, 4, 4, 128, width))
    back = back.reshape(degrees, 2, half, width)[:, :, :real].reshape(degrees, 2, samples, orders, width)
    return back.transpose(1, 2, 0, 3, 4), wgrad


def solution(mesh):
    placed = (
        P(),
        P(None, None, None, "order", "chan"),
        P(None, None, None, "order", "chan"),
        P(None, None, "chan"),
    )
    return jax.shard_map(
        per_device,
        mesh=mesh,
        in_specs=placed,
        out_specs=(P(None, None, None, "order", "chan"), P(None, "order", "chan")),
        check_vma=False,
    )
```

```python
import functools

import jax
import jax.numpy as jnp
from jax import lax
from jax.experimental import pallas as pl
from jax.experimental.pallas import tpu as pltpu
from jax.sharding import PartitionSpec as P

MESH = pl.DeviceIdType.MESH
BF16, F32 = jnp.bfloat16, jnp.float32

NX, NY, NZ = 4, 4, 4
NB = 8


def coords():
    order, chan = lax.axis_index("order"), lax.axis_index("chan")
    return order // 8, (order // 2) % 4, order % 2, chan // 4, chan % 4


def lanes(block):
    return pl.ds(pl.multiple_of(block * 128, 128), 128)


def kernel(
    orders, rows, window_ref, x_hbm, g_hbm, w_ref, back_ref, wgrad_ref,
    x_in, g_in, x_ref, g_ref, xz, xc, xt, gx, gp, gz, wt, acc, pair, part, relay, heap, fin, ret, wg,
    xa_s, xa_r, xc_r, xc_s, xt_r, ga_s, ga_r, gi_s, gi_r, w_s, w_r, w_loc,
    xr_s, xl_s, xz_r, gr_s, gl_s, gz_r, gx_s, gx_r,
    pair_s, pair_r, wo_s, wo_r, far_s, far_r, rs_s, rs_r, rt_s, rt_r, in_s, out_s,
):
    zh, y, k, x, zl = coords()
    z = zh * 4 + zl
    half = rows // 2
    me = y * 2 + k

    def dev(zh_, y_, k_, x_, zl_):
        return (zh_ * 8 + y_ * 2 + k_, x_ * 4 + zl_)

    def at_z(z_):
        return dev(z_ // 4, y, k, x, z_ % 4)

    def greet(device):
        pl.semaphore_signal(pltpu.get_barrier_semaphore(), inc=1, device_id=device, device_id_type=MESH)

    x_load = pltpu.make_async_copy(x_hbm, x_in, in_s.at[0])
    g_load = pltpu.make_async_copy(g_hbm, g_in, in_s.at[1])
    g_load.start()
    x_load.start()

    def greet_half(t, _):
        greet((zh * 8 + (me + t) % 8, x * 4 + zl))
        return 0

    lax.fori_loop(1, 8, greet_half, 0)

    @pl.when(zh != k)
    def _():
        def greet_other(t, _):
            greet(((1 - zh) * 8 + (me + t) % 8, x * 4 + zl))
            return 0

        lax.fori_loop(0, 8, greet_other, 0)

    for d in (1, 2, 6, 7):
        greet(at_z((z + d) % 8))
    for d in (1, 2, 3):
        for other in (0, 1):
            greet(dev(zh, y, other, (x + d) % 4, zl))

    def by_degree(raw, out):
        step = half // raw.shape[1]
        shape = (raw.shape[3], raw.shape[2], 128)
        degree_of = window_ref[0] + lax.broadcasted_iota(jnp.int32, shape, 0)
        order_of = (zh * 8 + me) * orders + lax.broadcasted_iota(jnp.int32, shape, 1)
        live = jnp.where(order_of <= degree_of, 1.0, 0.0)
        pad = jnp.zeros((shape[0], step - shape[1], 128), F32)
        for part_ in range(raw.shape[0]):
            for sample in range(raw.shape[1]):
                values = jnp.swapaxes(raw[part_, sample].astype(F32), 0, 1) * live
                at = pl.ds(part_ * half + sample * step, step)
                out[:, at] = jnp.concatenate([values, pad], axis=1).astype(BF16)

    g_load.wait()
    by_degree(g_in, g_ref)
    x_load.wait()
    by_degree(x_in, x_ref)
    pl.semaphore_wait(pltpu.get_barrier_semaphore(), 7 + 4 + 4 + 6)

    def remote(src, dst, send, recv, device):
        return pltpu.make_async_remote_copy(
            src_ref=src, dst_ref=dst, send_sem=send, recv_sem=recv, device_id=device, device_id_type=MESH
        )

    def blk(buf, b, lane):
        return buf.at[b, :, lanes(lane)]

    def to_weight(src, buf, lane, send, recv, t):
        e = (zh * 4 + y + t) % 8
        remote(src.at[e], blk(buf, me, lane), send.at[e], recv.at[me], dev(e // 4, e % 4, zh, x, zl)).start()

    def own_weight(src, buf, lane, recv, e):
        pltpu.make_async_copy(src.at[e], blk(buf, me, lane), recv.at[me]).start()

    def weight_out(src, buf, lane, send, recv):
        mine = zh == k

        @pl.when(mine)
        def _():
            own_weight(src, buf, lane, recv, zh * 4 + y)

        @pl.when(jnp.logical_not(mine))
        def _():
            to_weight(src, buf, lane, send, recv, 0)

        def step(t, _):
            to_weight(src, buf, lane, send, recv, t)
            return 0

        lax.fori_loop(1, 8, step, 0)

    def to_input(t):
        j = (me + t) % 8
        y_, k_ = j // 2, j % 2
        return remote(g_ref.at[4 * k_ + y_], blk(gz, me, zl), gi_s.at[j], gi_r.at[me], dev(zh, y_, k_, x, zl))

    def gi_step(t, _):
        to_input(t).start()
        return 0

    lax.fori_loop(1, 8, gi_step, 0)
    degree = 4 * k + y
    pltpu.make_async_copy(g_ref.at[degree], blk(gz, me, zl), gi_r.at[me]).start()
    source = zh == k

    def x_out(t, _):
        y_ = (y + t) % 4
        mine, other = zh * 4 + y_, (1 - zh) * 4 + y_
        itself = jnp.logical_and(source, t == 0)

        @pl.when(itself)
        def _():
            pltpu.make_async_copy(x_ref.at[mine], blk(xz, me, zl), xa_r.at[me]).start()
            pltpu.make_async_copy(x_ref.at[other], xc.at[me], xc_r.at[me]).start()

        @pl.when(jnp.logical_not(itself))
        def _():
            to = dev(zh, y_, zh, x, zl)
            remote(x_ref.at[mine], blk(xz, me, zl), xa_s.at[mine], xa_r.at[me], to).start()
            remote(x_ref.at[other], xc.at[me], xa_s.at[other], xc_r.at[me], to).start()

        return 0

    lax.fori_loop(0, 4, x_out, 0)

    weight_out(g_ref, gx, x, ga_s, ga_r)

    w_loc_copy = pltpu.make_async_copy(w_ref.at[:, degree, :, zl], wt.at[:, :, :, lanes(zl)], w_loc)
    w_loc_copy.start()
    w_copies = []
    for i, (d, part_of) in enumerate(((1, (0, 2)), (7, (0, 2)), (2, (0, 1)), (6, (1, 1)))):
        to = (z + d) % 8
        reim = pl.ds(*part_of)
        w_copies.append(
            remote(w_ref.at[reim, degree, :, to % 4], wt.at[reim, :, :, lanes(zl)], w_s.at[i], w_r.at[i], at_z(to))
        )
        w_copies[-1].start()

    def right(buf, o, b, send, recv):
        return remote(blk(buf, b, o), blk(buf, b, o), send.at[o, b], recv.at[o, b], dev(zh, y, k, x, (zl + 1) % 4))

    def left(buf, o, b, send, recv):
        return remote(blk(buf, b, o), blk(buf, b, o), send.at[o, b], recv.at[o, b], dev(zh, y, k, x, (zl + 3) % 4))

    def own_line(buf, b, s_r, s_l, recv):
        @pl.when(zl < 3)
        def _():
            right(buf, zl, b, s_r, recv).start()

        @pl.when(zl > 0)
        def _():
            left(buf, zl, b, s_l, recv).start()

    def pass_line(buf, b, d, s_r, s_l, recv):
        @pl.when(zl >= d)
        def _():
            o = zl - d
            right(buf, o, b, s_r, recv).wait_recv()

            @pl.when(zl < 3)
            def _():
                right(buf, o, b, s_r, recv).start()

        @pl.when(zl + d <= 3)
        def _():
            o = zl + d
            left(buf, o, b, s_l, recv).wait_recv()

            @pl.when(zl > 0)
            def _():
                left(buf, o, b, s_l, recv).start()

    def drain_line(buf, b, s_r, s_l, recv):
        for d in range(3):
            @pl.when((zl >= d) & (zl < 3))
            def _():
                right(buf, zl - d, b, s_r, recv).wait_send()

            @pl.when((zl + d <= 3) & (zl > 0))
            def _():
                left(buf, zl + d, b, s_l, recv).wait_send()

    def ring_right(o, b):
        return remote(blk(gx, b, o), blk(gx, b, o), gx_s.at[0, b], gx_r.at[0, b], dev(zh, y, k, (x + 1) % 4, zl))

    def ring_left(o, b):
        return remote(blk(gx, b, o), blk(gx, b, o), gx_s.at[1, b], gx_r.at[1, b], dev(zh, y, k, (x + 3) % 4, zl))

    def ring_far(to_right, b):
        o, to = ((x + 3) % 4, (x + 1) % 4) if to_right else ((x + 1) % 4, (x + 3) % 4)
        return remote(blk(gx, b, o), blk(gx, b, o), gx_s.at[2, b], gx_r.at[2, b], dev(zh, y, k, to, zl))

    def pair_of(c):
        return (2 * c, 2 * c + 1)

    def g_own(c):
        for b in pair_of(c):
            pltpu.make_async_copy(g_ref.at[0], blk(gz, b, zl), gi_r.at[b]).wait()
            own_line(gz, b, gr_s, gl_s, gz_r)

    def g_pass(c, d):
        for b in pair_of(c):
            pass_line(gz, b, d, gr_s, gl_s, gz_r)

    def x_right(src, o, b, send):
        return remote(src, blk(xz, b, o), send, xz_r.at[o, b], at_z((z + 1) % 8))

    def x_left(src, o, b, send):
        return remote(src, blk(xz, b, o), send, xz_r.at[o, b], at_z((z + 7) % 8))

    def transit(b, d):
        return remote(xc.at[b], xt.at[b], xc_s.at[0, b], xt_r.at[b], at_z((z + d) % 8))

    def x_cross(b):
        @pl.when(zl == 3)
        def _():
            x_right(xc.at[b], 3, b, xc_s.at[0, b]).start()

        @pl.when(zl == 0)
        def _():
            x_left(xc.at[b], 0, b, xc_s.at[0, b]).start()

        @pl.when(zl == 2)
        def _():
            transit(b, 1).start()

        @pl.when(zl == 1)
        def _():
            transit(b, 7).start()

    def x_transit(b):
        @pl.when(zl == 3)
        def _():
            transit(b, 1).wait_recv()
            x_right(xt.at[b], 2, b, xc_s.at[1, b]).start()

        @pl.when(zl == 0)
        def _():
            transit(b, 7).wait_recv()
            x_left(xt.at[b], 1, b, xc_s.at[1, b]).start()

    def x_own(c):
        @pl.when(source)
        def _():
            for b in pair_of(c):
                pltpu.make_async_copy(x_ref.at[0], blk(xz, b, zl), xa_r.at[b]).wait()
                own_line(xz, b, xr_s, xl_s, xz_r)

    def x_arrive(b, o, to_right):
        if to_right:
            x_right(blk(xz, b, o), o, b, xr_s.at[o, b]).wait_recv()

            @pl.when(zl < 3)
            def _():
                x_right(blk(xz, b, o), o, b, xr_s.at[o, b]).start()
        else:
            x_left(blk(xz, b, o), o, b, xl_s.at[o, b]).wait_recv()

            @pl.when(zl > 0)
            def _():
                x_left(blk(xz, b, o), o, b, xl_s.at[o, b]).start()

    def x_start(c):
        @pl.when(source)
        def _():
            for b in pair_of(c):
                pltpu.make_async_copy(x_ref.at[0], xc.at[b], xc_r.at[b]).wait()
                x_cross(b)

    def x_round(c, hops):
        if hops == 1:
            @pl.when(source)
            def _():
                for b in pair_of(c):
                    x_transit(b)

        @pl.when(jnp.logical_not(source))
        def _():
            for b in pair_of(c):
                for o, first in ((3, zl + 1), (2, zl + 2), (0, 4 - zl), (1, 5 - zl)):
                    @pl.when(first == hops)
                    def _():
                        x_arrive(b, o, o >= 2)

    def x_pass(c, d):
        @pl.when(source)
        def _():
            for b in pair_of(c):
                pass_line(xz, b, d, xr_s, xl_s, xz_r)

    def ring_own(c):
        for b in pair_of(c):
            pltpu.make_async_copy(g_ref.at[0], blk(gx, b, x), ga_r.at[b]).wait()
            ring_right(x, b).start()
            ring_left(x, b).start()

    def ring_pass(c):
        even, odd = pair_of(c)
        for b in (even, odd):
            ring_right((x + 3) % 4, b).wait_recv()
            ring_left((x + 1) % 4, b).wait_recv()
        ring_far(True, even).start()
        ring_far(False, odd).start()

    def ring_end(c):
        even, odd = pair_of(c)
        ring_far(True, even).wait_recv()
        ring_far(False, odd).wait_recv()
        cot = gx[pl.ds(2 * c, 2)]
        gp[pl.ds(2 * c, 2), 0:half] = cot[:, half:]
        gp[pl.ds(2 * c, 2), half:rows] = -cot[:, :half]

    def far(way, c):
        x_ = (x + 2) % 4
        at = pl.ds(0, half) if way == 0 else pl.ds(half, half)
        return remote(
            part.at[x_, pl.ds(2 * c, 2), at], relay.at[way, pl.ds(2 * c, 2)], far_s.at[way, c], far_r.at[way, c],
            dev(zh, y, k, (x + 1 + 2 * way) % 4, zl),
        )

    def near(way, c):
        x_ = (x + 1 + 2 * way) % 4
        return remote(
            part.at[x_, pl.ds(2 * c, 2)], heap.at[way, pl.ds(2 * c, 2)], rs_s.at[way, c], rs_r.at[way, c],
            dev(zh, y, k, x_, zl),
        )

    def back_relay(c):
        for way in (0, 1):
            far(way, c).wait_recv()
            x_ = (x + 1 + 2 * way) % 4
            for b in pair_of(c):
                if way == 0:
                    part[x_, b, 0:half] = part[x_, b, 0:half] + relay[way, b]
                else:
                    part[x_, b, half:rows] = part[x_, b, half:rows] + relay[way, b]
            near(way, c).start()

    def home(b):
        y_, k_ = b // 2, b % 2
        return remote(fin.at[b], ret.at[degree], rt_s.at[b], rt_r.at[degree], dev(zh, y_, k_, x, zl))

    def back_reduce(c):
        for way in (0, 1):
            near(way, c).wait_recv()
        for b in pair_of(c):
            fin[b] = part[x, b] + (heap[0, b] + heap[1, b])

            @pl.when(b == me)
            def _():
                pltpu.make_async_copy(fin.at[b], ret.at[degree], rt_r.at[degree]).start()

            @pl.when(b != me)
            def _():
                home(b).start()

    def back_product(c):
        cot = gz[pl.ds(2 * c, 2)].reshape(2 * rows, 512)
        over_lanes = (((1,), (1,)), ((), ()))
        by_re = lax.dot_general(cot, wt[0].reshape(512, 512), over_lanes, preferred_element_type=F32)
        by_im = lax.dot_general(cot, wt[1].reshape(512, 512), over_lanes, preferred_element_type=F32)
        for j in range(2):
            lo, mid, hi = j * rows, j * rows + half, (j + 1) * rows
            back_re = by_re[lo:mid] + by_im[mid:hi]
            back_im = by_re[mid:hi] - by_im[lo:mid]
            for x_ in range(NX):
                part[x_, 2 * c + j, 0:half] = back_re[:, x_ * 128 : (x_ + 1) * 128]
                part[x_, 2 * c + j, half:rows] = back_im[:, x_ * 128 : (x_ + 1) * 128]
        for way in (0, 1):
            far(way, c).start()

    def nth(t):
        if t == 0:
            return zl
        if t == 1:
            return zl + 1 - 2 * (zl % 2)
        return jnp.where(zl < 2, t, 3 - t)

    def swap(o):
        return remote(acc.at[1 - k, o], pair.at[o], pair_s.at[o], pair_r.at[o], dev(zh, y, 1 - k, x, zl))

    def owner_rows(o):
        return pl.ds(pl.multiple_of((x % 2) * 512 + o * 128, 128), 128)

    def wgrad_to(d, o):
        return remote(
            acc.at[k, o, :, lanes((x + d) % 4)], wg.at[k, owner_rows(o)],
            wo_s.at[d, o], wo_r.at[x % 2, k, o], dev(zh, y, x // 2, (x + d) % 4, zl),
        )

    def wgrad_product(t):
        o = nth(t)

        left_ = xz[:, :, lanes(o)].reshape(NB * rows, 128)
        over_rows = (((0,), (0,)), ((), ()))
        acc[0, o] = lax.dot_general(left_, gx[...].reshape(NB * rows, 512), over_rows, preferred_element_type=F32)
        acc[1, o] = lax.dot_general(left_, gp[...].reshape(NB * rows, 512), over_rows, preferred_element_type=F32)
        swap(o).start()

    def wgrad_send(t):
        o = nth(t)
        swap(o).wait_recv()
        acc[k, o] = acc[k, o] + pair[o]
        for d in (1, 3, 2):
            wgrad_to(d, o).start()

        @pl.when(k == x // 2)
        def _():
            pltpu.make_async_copy(
                acc.at[k, o, :, lanes(x)], wg.at[k, owner_rows(o)], wo_r.at[x % 2, k, o]
            ).start()

        @pl.when(k != x // 2)
        def _():
            wgrad_to(0, o).start()

    def when_chunk(c, work):
        @pl.when((c >= 0) & (c < 4))
        def _():
            work(c)

    def pipeline(s, _):
        when_chunk(s, g_own)
        when_chunk(s, x_start)
        when_chunk(s - 1, lambda c: g_pass(c, 1))
        when_chunk(s - 1, lambda c: x_round(c, 1))
        when_chunk(s - 1, ring_own)
        when_chunk(s - 2, lambda c: g_pass(c, 2))
        when_chunk(s - 2, lambda c: x_round(c, 2))

        @pl.when(s == 3)
        def _():
            w_loc_copy.wait()
            for copy in w_copies:
                copy.wait_recv()

        def product(c):
            g_pass(c, 3)
            back_product(c)

        when_chunk(s - 3, product)
        when_chunk(s - 3, x_own)
        when_chunk(s - 3, lambda c: x_round(c, 3))
        when_chunk(s - 2, ring_pass)
        when_chunk(s - 4, back_relay)
        when_chunk(s - 4, lambda c: x_round(c, 4))
        when_chunk(s - 3, ring_end)
        when_chunk(s - 5, lambda c: x_round(c, 5))
        when_chunk(s - 5, back_reduce)
        return 0

    def every(work):
        def step(c, _):
            work(c)
            return 0

        lax.fori_loop(0, 4, step, 0)

    lax.fori_loop(0, 7, pipeline, 0)
    x_round(3, 4)
    x_round(2, 5)
    x_round(3, 5)
    every(lambda c: x_pass(c, 1))
    back_relay(3)
    wgrad_product(0)
    back_reduce(2)
    wgrad_product(1)
    wgrad_send(0)
    every(lambda c: x_pass(c, 2))
    wgrad_product(2)
    wgrad_send(1)
    back_reduce(3)
    every(lambda c: x_pass(c, 3))
    wgrad_product(3)
    wgrad_send(2)
    wgrad_send(3)

    def returned(l, _):
        pltpu.make_async_copy(fin.at[0], ret.at[l], rt_r.at[l]).wait()
        return 0

    lax.fori_loop(0, NB, returned, 0)
    back_out = pltpu.make_async_copy(ret, back_ref, out_s.at[1])
    back_out.start()

    def owned(o, _):
        for r in range(2):
            for k_ in range(2):
                at = pl.ds(pl.multiple_of(r * 512 + o * 128, 128), 128)
                pltpu.make_async_copy(acc.at[0, 0, :, pl.ds(0, 128)], wg.at[k_, at], wo_r.at[r, k_, o]).wait()
        return 0

    lax.fori_loop(0, NZ, owned, 0)
    wg_out = pltpu.make_async_copy(wg, wgrad_ref, out_s.at[0])
    wg_out.start()

    def drain(b, _):
        @pl.when(source)
        def _():
            drain_line(xz, b, xr_s, xl_s, xz_r)
            x_right(xc.at[b], 3, b, xc_s.at[0, b]).wait_send()

            @pl.when((zl == 0) | (zl == 3))
            def _():
                x_right(xt.at[b], 2, b, xc_s.at[1, b]).wait_send()

        @pl.when(jnp.logical_not(source))
        def _():
            for o in (0, 1, 2, 3):
                if o >= 2:
                    @pl.when(zl < 3)
                    def _():
                        x_right(blk(xz, b, o), o, b, xr_s.at[o, b]).wait_send()
                else:
                    @pl.when(zl > 0)
                    def _():
                        x_left(blk(xz, b, o), o, b, xl_s.at[o, b]).wait_send()

        drain_line(gz, b, gr_s, gl_s, gz_r)
        for send in (0, 1, 2):
            remote(blk(gx, b, x), blk(gx, b, x), gx_s.at[send, b], gx_r.at[0, b], dev(zh, y, 1 - k, x, zl)).wait_send()

        @pl.when(jnp.logical_or(zh != k, b != zh * 4 + y))
        def _():
            pltpu.make_async_copy(g_ref.at[b], blk(gx, 0, x), ga_s.at[b]).wait()

        @pl.when(jnp.logical_or(zh != k, b % 4 != y))
        def _():
            pltpu.make_async_copy(x_ref.at[b], blk(xz, 0, zl), xa_s.at[b]).wait()

        @pl.when(b != me)
        def _():
            pltpu.make_async_copy(g_ref.at[0], blk(gz, 0, zl), gi_s.at[b]).wait()
            home(b).wait_send()

        return 0

    lax.fori_loop(0, NB, drain, 0)

    def drain_scatter(c, _):
        for way in (0, 1):
            far(way, c).wait_send()
            near(way, c).wait_send()
        return 0

    lax.fori_loop(0, NB // 2, drain_scatter, 0)
    for copy in w_copies:
        copy.wait_send()

    def drain_wgrad(o, _):
        swap(o).wait_send()
        for d in (1, 2, 3):
            wgrad_to(d, o).wait_send()

        @pl.when(k != x // 2)
        def _():
            wgrad_to(0, o).wait_send()

        return 0

    lax.fori_loop(0, NZ, drain_wgrad, 0)

    wg_out.wait()
    back_out.wait()


def per_device(window, inputs, out_grad, weights):
    _, samples, degrees, orders, width = inputs.shape
    step = -(-orders // 16) * 16
    half = samples * step
    rows = 2 * half

    dma, vmem = pltpu.SemaphoreType.DMA, pltpu.VMEM
    back, wgrad = pl.pallas_call(
        functools.partial(kernel, orders, rows),
        name="mix_back",
        out_shape=(
            jax.ShapeDtypeStruct((degrees, rows, width), F32),
            jax.ShapeDtypeStruct((2, 1024, width), F32),
        ),
        in_specs=[
            pl.BlockSpec(memory_space=pltpu.SMEM),
            pl.BlockSpec(memory_space=pl.ANY),
            pl.BlockSpec(memory_space=pl.ANY),
            pl.BlockSpec(memory_space=pl.ANY),
        ],
        out_specs=(pl.BlockSpec(memory_space=pl.ANY), pl.BlockSpec(memory_space=pl.ANY)),
        scratch_shapes=[
            vmem((2, samples, orders, degrees, width), BF16),
            vmem((2, samples, orders, degrees, width), BF16),
            vmem((degrees, rows, width), BF16),
            vmem((degrees, rows, width), BF16),
            vmem((NB, rows, 512), BF16),
            vmem((NB, rows, 128), BF16),
            vmem((NB, rows, 128), BF16),
            vmem((NB, rows, 512), BF16),
            vmem((NB, rows, 512), BF16),
            vmem((NB, rows, 512), BF16),
            vmem((2, 4, 128, 512), BF16),
            vmem((2, NZ, 128, 512), F32),
            vmem((NZ, 128, 512), F32),
            vmem((NX, NB, rows, 128), F32),
            vmem((2, NB, half, 128), F32),
            vmem((2, NB, rows, 128), F32),
            vmem((NB, rows, 128), F32),
            vmem((NB, rows, 128), F32),
            vmem((2, 1024, 128), F32),
            dma((8,)), dma((8,)), dma((8,)), dma((2, 8)), dma((8,)),
            dma((8,)), dma((8,)), dma((8,)), dma((8,)), dma((4,)), dma((4,)), dma(()),
            dma((4, 8)), dma((4, 8)), dma((4, 8)), dma((4, 8)), dma((4, 8)), dma((4, 8)), dma((3, 8)), dma((3, 8)),
            dma((4,)), dma((4,)), dma((4, 4)), dma((2, 2, 4)), dma((2, 4)), dma((2, 4)), dma((2, 4)), dma((2, 4)), dma((8,)), dma((8,)), dma((2,)), dma((2,)),
        ],
        compiler_params=pltpu.CompilerParams(
            collective_id=0, has_side_effects=True, vmem_limit_bytes=44 * 2**20
        ),
    )(
        window,
        inputs.transpose(0, 1, 3, 2, 4),
        out_grad.transpose(0, 1, 3, 2, 4),
        weights.reshape(2, degrees, 4, 4, 128, width),
    )
    back = back.reshape(degrees, 2, samples, step, width)[:, :, :, :orders]
    return back.transpose(1, 2, 0, 3, 4), wgrad


def solution(mesh):
    placed = (
        P(),
        P(None, None, None, "order", "chan"),
        P(None, None, None, "order", "chan"),
        P(None, None, "chan"),
    )
    return jax.shard_map(
        per_device,
        mesh=mesh,
        in_specs=placed,
        out_specs=(P(None, None, None, "order", "chan"), P(None, "order", "chan")),
        check_vma=False,
    )
```

```python
import functools

import jax
import jax.numpy as jnp
from jax import lax
from jax.experimental import pallas as pl
from jax.experimental.pallas import tpu as pltpu
from jax.sharding import PartitionSpec as P

MESH = pl.DeviceIdType.MESH
BF16, F32 = jnp.bfloat16, jnp.float32

NX, NY, NZ = 4, 4, 4
NB = 8


def coords():
    order, chan = lax.axis_index("order"), lax.axis_index("chan")
    return order // 8, (order // 2) % 4, order % 2, chan // 4, chan % 4


def lanes(block):
    return pl.ds(pl.multiple_of(block * 128, 128), 128)


def kernel(
    orders, rows, window_ref, x_hbm, g_hbm, w_ref, back_ref, wgrad_ref,
    x_in, g_in, x_ref, g_ref, xz, xc, xt, gx, gp, gz, wt, acc, pair, part, relay, heap, fin,
    xa_s, xa_r, xc_r, xc_s, xt_r, gc_s, gc_r, gi_s, gi_r, w_s, w_r, w_loc,
    xr_s, xl_s, xz_r, gr_s, gl_s, gz_r, gx_s, gx_r,
    pair_s, pair_r, wo_s, wo_r, far_s, far_r, rs_s, rs_r, rt_s, rt_r, in_s,
):
    zh, y, k, x, zl = coords()
    z = zh * 4 + zl
    half = rows // 2
    me = y * 2 + k

    def dev(zh_, y_, k_, x_, zl_):
        return (zh_ * 8 + y_ * 2 + k_, x_ * 4 + zl_)

    def at_z(z_):
        return dev(z_ // 4, y, k, x, z_ % 4)

    def greet(device):
        pl.semaphore_signal(pltpu.get_barrier_semaphore(), inc=1, device_id=device, device_id_type=MESH)

    x_load = pltpu.make_async_copy(x_hbm, x_in, in_s.at[0])
    g_load = pltpu.make_async_copy(g_hbm, g_in, in_s.at[1])
    g_load.start()
    x_load.start()

    def greet_half(t, _):
        greet((zh * 8 + (me + t) % 8, x * 4 + zl))
        return 0

    lax.fori_loop(1, 8, greet_half, 0)

    @pl.when(zh != k)
    def _():
        end = jnp.where(zl < 2, 7 - zl, 4 - zl)
        z_ = (z + end) % 8
        greet(dev(z_ // 4, y, 1 - k, x, z_ % 4))

    for d in (1, 2, 6, 7):
        greet(at_z((z + d) % 8))
    for d in (1, 2, 3):
        for other in (0, 1):
            greet(dev(zh, y, other, (x + d) % 4, zl))

    def by_degree(raw, out):
        step = half // raw.shape[1]
        shape = (raw.shape[3], raw.shape[2], 128)
        degree_of = window_ref[0] + lax.broadcasted_iota(jnp.int32, shape, 0)
        order_of = (zh * 8 + me) * orders + lax.broadcasted_iota(jnp.int32, shape, 1)
        live = jnp.where(order_of <= degree_of, 1.0, 0.0)
        pad = jnp.zeros((shape[0], step - shape[1], 128), F32)
        for part_ in range(raw.shape[0]):
            for sample in range(raw.shape[1]):
                values = jnp.swapaxes(raw[part_, sample].astype(F32), 0, 1) * live
                at = pl.ds(part_ * half + sample * step, step)
                out[:, at] = jnp.concatenate([values, pad], axis=1).astype(BF16)

    g_load.wait()
    by_degree(g_in, g_ref)
    x_load.wait()
    by_degree(x_in, x_ref)
    at_end = jnp.logical_and(zh != k, jnp.logical_or(zl == 0, zl == 3))

    @pl.when(at_end)
    def _():
        pl.semaphore_wait(pltpu.get_barrier_semaphore(), 7 + 4 + 6 + 2)

    @pl.when(jnp.logical_not(at_end))
    def _():
        pl.semaphore_wait(pltpu.get_barrier_semaphore(), 7 + 4 + 6)


    def remote(src, dst, send, recv, device):
        return pltpu.make_async_remote_copy(
            src_ref=src, dst_ref=dst, send_sem=send, recv_sem=recv, device_id=device, device_id_type=MESH
        )

    def blk(buf, b, lane):
        return buf.at[b, :, lanes(lane)]

    def two(buf, c, lane):
        return buf.at[pl.ds(2 * c, 2), :, lanes(lane)]

    def to_input(t):
        j = (me + t) % 8
        y_, k_ = j // 2, j % 2
        return remote(g_ref.at[4 * k_ + y_], blk(gz, me, zl), gi_s.at[j], gi_r.at[me], dev(zh, y_, k_, x, zl))

    def gi_step(t, _):
        to_input(t).start()
        return 0

    lax.fori_loop(1, 8, gi_step, 0)
    degree = 4 * k + y
    pltpu.make_async_copy(g_ref.at[degree], blk(gz, me, zl), gi_r.at[me]).start()
    source = zh == k

    def x_out(t, _):
        y_ = (y + t) % 4
        mine, other = zh * 4 + y_, (1 - zh) * 4 + y_
        itself = jnp.logical_and(source, t == 0)

        @pl.when(itself)
        def _():
            pltpu.make_async_copy(x_ref.at[mine], blk(xz, me, zl), xa_r.at[me]).start()
            pltpu.make_async_copy(x_ref.at[other], xc.at[me], xc_r.at[me]).start()

        @pl.when(jnp.logical_not(itself))
        def _():
            to = dev(zh, y_, zh, x, zl)
            remote(x_ref.at[mine], blk(xz, me, zl), xa_s.at[mine], xa_r.at[me], to).start()
            remote(x_ref.at[other], xc.at[me], xa_s.at[other], xc_r.at[me], to).start()

        return 0

    lax.fori_loop(0, 4, x_out, 0)


    w_loc_copy = pltpu.make_async_copy(w_ref.at[:, degree, :, zl], wt.at[:, :, :, lanes(zl)], w_loc)
    w_loc_copy.start()
    w_copies = []
    for i, (d, part_of) in enumerate(((1, (0, 2)), (7, (0, 2)), (2, (0, 1)), (6, (1, 1)))):
        to = (z + d) % 8
        reim = pl.ds(*part_of)
        w_copies.append(
            remote(w_ref.at[reim, degree, :, to % 4], wt.at[reim, :, :, lanes(zl)], w_s.at[i], w_r.at[i], at_z(to))
        )
        w_copies[-1].start()

    def right(buf, o, c, send, recv):
        return remote(two(buf, c, o), two(buf, c, o), send.at[o, c], recv.at[o, c], dev(zh, y, k, x, (zl + 1) % 4))

    def left(buf, o, c, send, recv):
        return remote(two(buf, c, o), two(buf, c, o), send.at[o, c], recv.at[o, c], dev(zh, y, k, x, (zl + 3) % 4))

    def own_line(buf, c, s_r, s_l, recv):
        @pl.when(zl < 3)
        def _():
            right(buf, zl, c, s_r, recv).start()

        @pl.when(zl > 0)
        def _():
            left(buf, zl, c, s_l, recv).start()

    def pass_line(buf, c, d, s_r, s_l, recv):
        @pl.when(zl >= d)
        def _():
            o = zl - d
            right(buf, o, c, s_r, recv).wait_recv()

            @pl.when(zl < 3)
            def _():
                right(buf, o, c, s_r, recv).start()

        @pl.when(zl + d <= 3)
        def _():
            o = zl + d
            left(buf, o, c, s_l, recv).wait_recv()

            @pl.when(zl > 0)
            def _():
                left(buf, o, c, s_l, recv).start()

    def drain_line(buf, c, s_r, s_l, recv):
        for d in range(3):
            @pl.when((zl >= d) & (zl < 3))
            def _():
                right(buf, zl - d, c, s_r, recv).wait_send()

            @pl.when((zl + d <= 3) & (zl > 0))
            def _():
                left(buf, zl + d, c, s_l, recv).wait_send()

    def ring_right(o, c):
        return remote(two(gx, c, o), two(gx, c, o), gx_s.at[0, c], gx_r.at[0, c], dev(zh, y, k, (x + 1) % 4, zl))

    def ring_left(o, c):
        return remote(two(gx, c, o), two(gx, c, o), gx_s.at[1, c], gx_r.at[1, c], dev(zh, y, k, (x + 3) % 4, zl))

    def ring_far(to_right, b):
        o, to = ((x + 3) % 4, (x + 1) % 4) if to_right else ((x + 1) % 4, (x + 3) % 4)
        return remote(blk(gx, b, o), blk(gx, b, o), gx_s.at[2, b], gx_r.at[2, b], dev(zh, y, k, to, zl))

    def pair_of(c):
        return (2 * c, 2 * c + 1)

    def g_own(c):
        for b in pair_of(c):
            pltpu.make_async_copy(g_ref.at[0], blk(gz, b, zl), gi_r.at[b]).wait()
        own_line(gz, c, gr_s, gl_s, gz_r)

        @pl.when(source)
        def _():
            pltpu.make_async_copy(two(gz, c, zl), two(gx, c, x), gc_r.at[c]).start()

    def g_pass(c, d):
        pass_line(gz, c, d, gr_s, gl_s, gz_r)

    def x_right(src, o, c, send):
        return remote(src, two(xz, c, o), send, xz_r.at[o, c], at_z((z + 1) % 8))

    def x_left(src, o, c, send):
        return remote(src, two(xz, c, o), send, xz_r.at[o, c], at_z((z + 7) % 8))

    def transit(c, d):
        return remote(xc.at[pl.ds(2 * c, 2)], xt.at[pl.ds(2 * c, 2)], xc_s.at[0, c], xt_r.at[c], at_z((z + d) % 8))

    def x_cross(c):
        @pl.when(zl == 3)
        def _():
            x_right(xc.at[pl.ds(2 * c, 2)], 3, c, xc_s.at[0, c]).start()

        @pl.when(zl == 0)
        def _():
            x_left(xc.at[pl.ds(2 * c, 2)], 0, c, xc_s.at[0, c]).start()

        @pl.when(zl == 2)
        def _():
            transit(c, 1).start()

        @pl.when(zl == 1)
        def _():
            transit(c, 7).start()

    def x_transit(c):
        @pl.when(zl == 3)
        def _():
            transit(c, 1).wait_recv()
            x_right(xt.at[pl.ds(2 * c, 2)], 2, c, xc_s.at[1, c]).start()

        @pl.when(zl == 0)
        def _():
            transit(c, 7).wait_recv()
            x_left(xt.at[pl.ds(2 * c, 2)], 1, c, xc_s.at[1, c]).start()

    def x_own(c):
        @pl.when(source)
        def _():
            for b in pair_of(c):
                pltpu.make_async_copy(x_ref.at[0], blk(xz, b, zl), xa_r.at[b]).wait()
            own_line(xz, c, xr_s, xl_s, xz_r)

    def x_arrive(c, o, to_right):
        if to_right:
            x_right(two(xz, c, o), o, c, xr_s.at[o, c]).wait_recv()

            @pl.when(zl < 3)
            def _():
                x_right(two(xz, c, o), o, c, xr_s.at[o, c]).start()
        else:
            x_left(two(xz, c, o), o, c, xl_s.at[o, c]).wait_recv()

            @pl.when(zl > 0)
            def _():
                x_left(two(xz, c, o), o, c, xl_s.at[o, c]).start()

    def x_start(c):
        @pl.when(source)
        def _():
            for b in pair_of(c):
                pltpu.make_async_copy(x_ref.at[0], xc.at[b], xc_r.at[b]).wait()
            x_cross(c)

    def x_round(c, hops):
        if hops == 1:
            @pl.when(source)
            def _():
                x_transit(c)

        @pl.when(jnp.logical_not(source))
        def _():
            for o, first in ((3, zl + 1), (2, zl + 2), (0, 4 - zl), (1, 5 - zl)):
                @pl.when(first == hops)
                def _():
                    x_arrive(c, o, o >= 2)

    def x_pass(c, d):
        @pl.when(source)
        def _():
            pass_line(xz, c, d, xr_s, xl_s, xz_r)

    def g_cross(near, c):
        o = jnp.where(zl == 3, near, 3 - near)
        return remote(two(gz, c, o), two(gx, c, x), gc_s.at[near, c], gc_r.at[c], dev(1 - zh, y, zh, x, o))

    def g_over(c):
        @pl.when(at_end)
        def _():
            g_cross(0, c).start()
            g_cross(1, c).start()

    def ring_own(c):
        pltpu.make_async_copy(two(gz, c, zl), two(gx, c, x), gc_r.at[c]).wait()
        ring_right(x, c).start()
        ring_left(x, c).start()

    def ring_pass(c):
        even, odd = pair_of(c)
        ring_right((x + 3) % 4, c).wait_recv()
        ring_left((x + 1) % 4, c).wait_recv()
        ring_far(True, even).start()
        ring_far(False, odd).start()

    def ring_end(c):
        even, odd = pair_of(c)
        ring_far(True, even).wait_recv()
        ring_far(False, odd).wait_recv()
        cot = gx[pl.ds(2 * c, 2)]
        gp[pl.ds(2 * c, 2), 0:half] = cot[:, half:]
        gp[pl.ds(2 * c, 2), half:rows] = -cot[:, :half]

    def far(way, c):
        x_ = (x + 2) % 4
        at = pl.ds(0, half) if way == 0 else pl.ds(half, half)
        return remote(
            part.at[x_, pl.ds(2 * c, 2), at], relay.at[way, pl.ds(2 * c, 2)], far_s.at[way, c], far_r.at[way, c],
            dev(zh, y, k, (x + 1 + 2 * way) % 4, zl),
        )

    def near(way, c):
        x_ = (x + 1 + 2 * way) % 4
        return remote(
            part.at[x_, pl.ds(2 * c, 2)], heap.at[way, pl.ds(2 * c, 2)], rs_s.at[way, c], rs_r.at[way, c],
            dev(zh, y, k, x_, zl),
        )

    def back_relay(c):
        for way in (0, 1):
            far(way, c).wait_recv()
            x_ = (x + 1 + 2 * way) % 4
            for b in pair_of(c):
                if way == 0:
                    part[x_, b, 0:half] = part[x_, b, 0:half] + relay[way, b]
                else:
                    part[x_, b, half:rows] = part[x_, b, half:rows] + relay[way, b]
            near(way, c).start()

    def home(b):
        y_, k_ = b // 2, b % 2
        return remote(fin.at[b], back_ref.at[degree], rt_s.at[b], rt_r.at[degree], dev(zh, y_, k_, x, zl))

    def back_reduce(c):
        for way in (0, 1):
            near(way, c).wait_recv()
        for b in pair_of(c):
            fin[b] = part[x, b] + (heap[0, b] + heap[1, b])

            @pl.when(b == me)
            def _():
                pltpu.make_async_copy(fin.at[b], back_ref.at[degree], rt_r.at[degree]).start()

            @pl.when(b != me)
            def _():
                home(b).start()

    def back_product(c):
        cot = gz[pl.ds(2 * c, 2)].reshape(2 * rows, 512)
        over_lanes = (((1,), (1,)), ((), ()))
        by_re = lax.dot_general(cot, wt[0].reshape(512, 512), over_lanes, preferred_element_type=F32)
        by_im = lax.dot_general(cot, wt[1].reshape(512, 512), over_lanes, preferred_element_type=F32)
        for j in range(2):
            lo, mid, hi = j * rows, j * rows + half, (j + 1) * rows
            back_re = by_re[lo:mid] + by_im[mid:hi]
            back_im = by_re[mid:hi] - by_im[lo:mid]
            for x_ in range(NX):
                part[x_, 2 * c + j, 0:half] = back_re[:, x_ * 128 : (x_ + 1) * 128]
                part[x_, 2 * c + j, half:rows] = back_im[:, x_ * 128 : (x_ + 1) * 128]
        for way in (0, 1):
            far(way, c).start()

    def nth(t):
        if t == 0:
            return zl
        if t == 1:
            return zl + 1 - 2 * (zl % 2)
        return jnp.where(zl < 2, t, 3 - t)

    def swap(o):
        return remote(acc.at[1 - k, o], pair.at[o], pair_s.at[o], pair_r.at[o], dev(zh, y, 1 - k, x, zl))

    def owner_rows(o):
        return pl.ds(pl.multiple_of((x % 2) * 512 + o * 128, 128), 128)

    def wgrad_to(d, o):
        return remote(
            acc.at[k, o, :, lanes((x + d) % 4)], wgrad_ref.at[k, owner_rows(o)],
            wo_s.at[d, o], wo_r.at[x % 2, k, o], dev(zh, y, x // 2, (x + d) % 4, zl),
        )

    def wgrad_product(t):
        o = nth(t)

        left_ = xz[:, :, lanes(o)].reshape(NB * rows, 128)
        over_rows = (((0,), (0,)), ((), ()))
        acc[0, o] = lax.dot_general(left_, gx[...].reshape(NB * rows, 512), over_rows, preferred_element_type=F32)
        acc[1, o] = lax.dot_general(left_, gp[...].reshape(NB * rows, 512), over_rows, preferred_element_type=F32)
        swap(o).start()

    def wgrad_send(t):
        o = nth(t)
        swap(o).wait_recv()
        acc[k, o] = acc[k, o] + pair[o]
        for d in (1, 3, 2):
            wgrad_to(d, o).start()

        @pl.when(k == x // 2)
        def _():
            pltpu.make_async_copy(
                acc.at[k, o, :, lanes(x)], wgrad_ref.at[k, owner_rows(o)], wo_r.at[x % 2, k, o]
            ).start()

        @pl.when(k != x // 2)
        def _():
            wgrad_to(0, o).start()

    def when_chunk(c, work):
        @pl.when((c >= 0) & (c < 4))
        def _():
            work(c)

    def pipeline(s, _):
        when_chunk(s, g_own)
        when_chunk(s, x_start)
        when_chunk(s - 1, lambda c: g_pass(c, 1))
        when_chunk(s - 1, lambda c: x_round(c, 1))

        @pl.when(source)
        def _():
            when_chunk(s - 1, ring_own)

        when_chunk(s - 2, lambda c: g_pass(c, 2))
        when_chunk(s - 2, lambda c: x_round(c, 2))

        @pl.when(source)
        def _():
            when_chunk(s - 2, ring_pass)


        @pl.when(s == 3)
        def _():
            w_loc_copy.wait()
            for copy in w_copies:
                copy.wait_recv()

        def product(c):
            g_pass(c, 3)
            g_over(c)
            back_product(c)

        when_chunk(s - 3, product)
        when_chunk(s - 3, x_own)
        when_chunk(s - 3, lambda c: x_round(c, 3))
        when_chunk(s - 4, back_relay)
        when_chunk(s - 4, lambda c: x_round(c, 4))
        @pl.when(source)
        def _():
            when_chunk(s - 3, ring_end)

        @pl.when(jnp.logical_not(source))
        def _():
            when_chunk(s - 4, ring_own)
            when_chunk(s - 5, ring_pass)
            when_chunk(s - 6, ring_end)

        when_chunk(s - 5, lambda c: x_round(c, 5))
        when_chunk(s - 6, back_reduce)
        return 0

    def every(work):
        def step(c, _):
            work(c)
            return 0

        lax.fori_loop(0, 4, step, 0)

    lax.fori_loop(0, 7, pipeline, 0)
    x_round(3, 4)
    x_round(2, 5)
    x_round(3, 5)
    every(lambda c: x_pass(c, 1))

    @pl.when(jnp.logical_not(source))
    def _():
        ring_own(3)
        ring_pass(2)
        ring_end(1)
        ring_pass(3)
        ring_end(2)
        ring_end(3)

    back_relay(3)
    back_reduce(1)
    wgrad_product(0)
    wgrad_product(1)
    wgrad_send(0)
    every(lambda c: x_pass(c, 2))
    back_reduce(2)
    wgrad_product(2)
    wgrad_send(1)
    every(lambda c: x_pass(c, 3))
    wgrad_product(3)
    wgrad_send(2)
    wgrad_send(3)
    back_reduce(3)

    def drain_pairs(c, _):
        @pl.when(source)
        def _():
            drain_line(xz, c, xr_s, xl_s, xz_r)
            x_right(xc.at[pl.ds(2 * c, 2)], 3, c, xc_s.at[0, c]).wait_send()

            @pl.when((zl == 0) | (zl == 3))
            def _():
                x_right(xt.at[pl.ds(2 * c, 2)], 2, c, xc_s.at[1, c]).wait_send()

        @pl.when(jnp.logical_not(source))
        def _():
            for o in (0, 1, 2, 3):
                if o >= 2:
                    @pl.when(zl < 3)
                    def _():
                        x_right(two(xz, c, o), o, c, xr_s.at[o, c]).wait_send()
                else:
                    @pl.when(zl > 0)
                    def _():
                        x_left(two(xz, c, o), o, c, xl_s.at[o, c]).wait_send()

        drain_line(gz, c, gr_s, gl_s, gz_r)
        @pl.when(at_end)
        def _():
            g_cross(0, c).wait_send()
            g_cross(1, c).wait_send()

        ring_right(x, c).wait_send()
        ring_left(x, c).wait_send()
        return 0

    lax.fori_loop(0, 4, drain_pairs, 0)

    def drain(b, _):
        ring_far(True, b).wait_send()

        @pl.when(jnp.logical_or(zh != k, b % 4 != y))
        def _():
            pltpu.make_async_copy(x_ref.at[b], blk(xz, 0, zl), xa_s.at[b]).wait()

        @pl.when(b != me)
        def _():
            pltpu.make_async_copy(g_ref.at[0], blk(gz, 0, zl), gi_s.at[b]).wait()
            home(b).wait_send()

        return 0

    lax.fori_loop(0, NB, drain, 0)

    def drain_scatter(c, _):
        for way in (0, 1):
            far(way, c).wait_send()
            near(way, c).wait_send()
        return 0

    lax.fori_loop(0, NB // 2, drain_scatter, 0)
    for copy in w_copies:
        copy.wait_send()

    def returned(l, _):
        pltpu.make_async_copy(fin.at[0], back_ref.at[l], rt_r.at[l]).wait()
        return 0

    lax.fori_loop(0, NB, returned, 0)

    def owned(o, _):
        swap(o).wait_send()
        for d in (1, 2, 3):
            wgrad_to(d, o).wait_send()

        @pl.when(k != x // 2)
        def _():
            wgrad_to(0, o).wait_send()

        for r in range(2):
            for k_ in range(2):
                at = pl.ds(pl.multiple_of(r * 512 + o * 128, 128), 128)
                pltpu.make_async_copy(acc.at[0, 0, :, pl.ds(0, 128)], wgrad_ref.at[k_, at], wo_r.at[r, k_, o]).wait()
        return 0

    lax.fori_loop(0, NZ, owned, 0)


def per_device(window, inputs, out_grad, weights):
    _, samples, degrees, orders, width = inputs.shape
    step = -(-orders // 16) * 16
    half = samples * step
    rows = 2 * half

    dma, vmem = pltpu.SemaphoreType.DMA, pltpu.VMEM
    back, wgrad = pl.pallas_call(
        functools.partial(kernel, orders, rows),
        name="mix_back",
        out_shape=(
            jax.ShapeDtypeStruct((degrees, rows, width), F32),
            jax.ShapeDtypeStruct((2, 1024, width), F32),
        ),
        in_specs=[
            pl.BlockSpec(memory_space=pltpu.SMEM),
            pl.BlockSpec(memory_space=pl.ANY),
            pl.BlockSpec(memory_space=pl.ANY),
            pl.BlockSpec(memory_space=pl.ANY),
        ],
        out_specs=(pl.BlockSpec(memory_space=pl.ANY), pl.BlockSpec(memory_space=pl.ANY)),
        scratch_shapes=[
            vmem((2, samples, orders, degrees, width), BF16),
            vmem((2, samples, orders, degrees, width), BF16),
            vmem((degrees, rows, width), BF16),
            vmem((degrees, rows, width), BF16),
            vmem((NB, rows, 512), BF16),
            vmem((NB, rows, 128), BF16),
            vmem((NB, rows, 128), BF16),
            vmem((NB, rows, 512), BF16),
            vmem((NB, rows, 512), BF16),
            vmem((NB, rows, 512), BF16),
            vmem((2, 4, 128, 512), BF16),
            vmem((2, NZ, 128, 512), F32),
            vmem((NZ, 128, 512), F32),
            vmem((NX, NB, rows, 128), F32),
            vmem((2, NB, half, 128), F32),
            vmem((2, NB, rows, 128), F32),
            vmem((NB, rows, 128), F32),
            dma((8,)), dma((8,)), dma((8,)), dma((2, 4)), dma((4,)),
            dma((2, 4)), dma((4,)), dma((8,)), dma((8,)), dma((4,)), dma((4,)), dma(()),
            dma((4, 4)), dma((4, 4)), dma((4, 4)), dma((4, 4)), dma((4, 4)), dma((4, 4)), dma((3, 8)), dma((3, 8)),
            dma((4,)), dma((4,)), dma((4, 4)), dma((2, 2, 4)), dma((2, 4)), dma((2, 4)), dma((2, 4)), dma((2, 4)), dma((8,)), dma((8,)), dma((2,)),
        ],
        compiler_params=pltpu.CompilerParams(
            collective_id=0, has_side_effects=True, vmem_limit_bytes=44 * 2**20
        ),
    )(
        window,
        inputs.transpose(0, 1, 3, 2, 4),
        out_grad.transpose(0, 1, 3, 2, 4),
        weights.reshape(2, degrees, 4, 4, 128, width),
    )
    back = back.reshape(degrees, 2, samples, step, width)[:, :, :, :orders]
    return back.transpose(1, 2, 0, 3, 4), wgrad


def solution(mesh):
    placed = (
        P(),
        P(None, None, None, "order", "chan"),
        P(None, None, None, "order", "chan"),
        P(None, None, "chan"),
    )
    return jax.shard_map(
        per_device,
        mesh=mesh,
        in_specs=placed,
        out_specs=(P(None, None, None, "order", "chan"), P(None, "order", "chan")),
        check_vma=False,
    )
```

```python
import functools

import jax
import jax.numpy as jnp
from jax import lax
from jax.experimental import pallas as pl
from jax.experimental.pallas import tpu as pltpu
from jax.sharding import PartitionSpec as P

MESH = pl.DeviceIdType.MESH
BF16, F32 = jnp.bfloat16, jnp.float32

NX, NY, NZ = 4, 4, 4
NB = 8


def coords():
    order, chan = lax.axis_index("order"), lax.axis_index("chan")
    return order // 8, (order // 2) % 4, order % 2, chan // 4, chan % 4


def lanes(block):
    return pl.ds(pl.multiple_of(block * 128, 128), 128)


def kernel(
    orders, rows, window_ref, x_hbm, g_hbm, w_ref, back_ref, wgrad_ref,
    x_in, g_in, x_ref, g_ref, xz, xc, xt, gx, gp, gz, wt, acc, pair, part, relay, heap, fin,
    xa_s, xa_r, xc_r, xc_s, xt_r, gc_s, gc_r, gi_s, gi_r, w_s, w_r, w_loc,
    xr_s, xl_s, xz_r, gr_s, gl_s, gz_r, gx_s, gx_r,
    pair_s, pair_r, wo_s, wo_r, far_s, far_r, rs_s, rs_r, rt_s, rt_r, in_s,
):
    zh, y, k, x, zl = coords()
    z = zh * 4 + zl
    half = rows // 2
    me = y * 2 + k

    def dev(zh_, y_, k_, x_, zl_):
        return (zh_ * 8 + y_ * 2 + k_, x_ * 4 + zl_)

    def at_z(z_):
        return dev(z_ // 4, y, k, x, z_ % 4)

    def greet(device):
        pl.semaphore_signal(pltpu.get_barrier_semaphore(), inc=1, device_id=device, device_id_type=MESH)

    x_load = pltpu.make_async_copy(x_hbm, x_in, in_s.at[0])
    g_load = pltpu.make_async_copy(g_hbm, g_in, in_s.at[1])
    g_load.start()
    x_load.start()

    def greet_half(t, _):
        greet((zh * 8 + (me + t) % 8, x * 4 + zl))
        return 0

    lax.fori_loop(1, 8, greet_half, 0)

    @pl.when(zh != k)
    def _():
        end = jnp.where(zl < 2, 7 - zl, 4 - zl)
        z_ = (z + end) % 8
        greet(dev(z_ // 4, y, 1 - k, x, z_ % 4))

    for d in (1, 2, 6, 7):
        greet(at_z((z + d) % 8))
    for d in (1, 2, 3):
        for other in (0, 1):
            greet(dev(zh, y, other, (x + d) % 4, zl))

    def by_degree(raw, out):
        step = half // raw.shape[1]
        shape = (raw.shape[3], raw.shape[2], 128)
        degree_of = window_ref[0] + lax.broadcasted_iota(jnp.int32, shape, 0)
        order_of = (zh * 8 + me) * orders + lax.broadcasted_iota(jnp.int32, shape, 1)
        live = jnp.where(order_of <= degree_of, 1.0, 0.0)
        pad = jnp.zeros((shape[0], step - shape[1], 128), F32)
        for part_ in range(raw.shape[0]):
            for sample in range(raw.shape[1]):
                values = jnp.swapaxes(raw[part_, sample].astype(F32), 0, 1) * live
                at = pl.ds(part_ * half + sample * step, step)
                out[:, at] = jnp.concatenate([values, pad], axis=1).astype(BF16)

    g_load.wait()
    by_degree(g_in, g_ref)
    x_load.wait()
    by_degree(x_in, x_ref)
    at_end = jnp.logical_and(zh != k, jnp.logical_or(zl == 0, zl == 3))

    @pl.when(at_end)
    def _():
        pl.semaphore_wait(pltpu.get_barrier_semaphore(), 7 + 4 + 6 + 2)

    @pl.when(jnp.logical_not(at_end))
    def _():
        pl.semaphore_wait(pltpu.get_barrier_semaphore(), 7 + 4 + 6)


    def remote(src, dst, send, recv, device):
        return pltpu.make_async_remote_copy(
            src_ref=src, dst_ref=dst, send_sem=send, recv_sem=recv, device_id=device, device_id_type=MESH
        )

    def blk(buf, b, lane):
        return buf.at[b, :, lanes(lane)]

    def two(buf, c, lane):
        return buf.at[pl.ds(2 * c, 2), :, lanes(lane)]

    def to_input(t):
        j = (me + t) % 8
        y_, k_ = j // 2, j % 2
        return remote(g_ref.at[4 * k_ + y_], blk(gz, me, zl), gi_s.at[j], gi_r.at[me], dev(zh, y_, k_, x, zl))

    def gi_step(t, _):
        to_input(t).start()
        return 0

    lax.fori_loop(1, 8, gi_step, 0)
    degree = 4 * k + y
    pltpu.make_async_copy(g_ref.at[degree], blk(gz, me, zl), gi_r.at[me]).start()
    w_loc_copy = pltpu.make_async_copy(w_ref.at[:, degree, :, zl], wt.at[:, :, :, lanes(zl)], w_loc)
    w_loc_copy.start()
    w_copies = []
    for i, (d, part_of) in enumerate(((1, (0, 2)), (7, (0, 2)), (2, (0, 1)), (6, (1, 1)))):
        to = (z + d) % 8
        reim = pl.ds(*part_of)
        w_copies.append(
            remote(w_ref.at[reim, degree, :, to % 4], wt.at[reim, :, :, lanes(zl)], w_s.at[i], w_r.at[i], at_z(to))
        )
        w_copies[-1].start()

    source = zh == k

    def x_out(t, _):
        y_ = (y + t) % 4
        mine, other = zh * 4 + y_, (1 - zh) * 4 + y_
        itself = jnp.logical_and(source, t == 0)

        @pl.when(itself)
        def _():
            pltpu.make_async_copy(x_ref.at[mine], blk(xz, me, zl), xa_r.at[me]).start()
            pltpu.make_async_copy(x_ref.at[other], xc.at[me], xc_r.at[me]).start()

        @pl.when(jnp.logical_not(itself))
        def _():
            to = dev(zh, y_, zh, x, zl)
            remote(x_ref.at[mine], blk(xz, me, zl), xa_s.at[mine], xa_r.at[me], to).start()
            remote(x_ref.at[other], xc.at[me], xa_s.at[other], xc_r.at[me], to).start()

        return 0

    lax.fori_loop(0, 4, x_out, 0)


    def right(buf, o, c, send, recv):
        return remote(two(buf, c, o), two(buf, c, o), send.at[o, c], recv.at[o, c], dev(zh, y, k, x, (zl + 1) % 4))

    def left(buf, o, c, send, recv):
        return remote(two(buf, c, o), two(buf, c, o), send.at[o, c], recv.at[o, c], dev(zh, y, k, x, (zl + 3) % 4))

    def own_line(buf, c, s_r, s_l, recv):
        @pl.when(zl < 3)
        def _():
            right(buf, zl, c, s_r, recv).start()

        @pl.when(zl > 0)
        def _():
            left(buf, zl, c, s_l, recv).start()

    def pass_line(buf, c, d, s_r, s_l, recv):
        @pl.when(zl >= d)
        def _():
            o = zl - d
            right(buf, o, c, s_r, recv).wait_recv()

            @pl.when(zl < 3)
            def _():
                right(buf, o, c, s_r, recv).start()

        @pl.when(zl + d <= 3)
        def _():
            o = zl + d
            left(buf, o, c, s_l, recv).wait_recv()

            @pl.when(zl > 0)
            def _():
                left(buf, o, c, s_l, recv).start()

    def drain_line(buf, c, s_r, s_l, recv):
        for d in range(3):
            @pl.when((zl >= d) & (zl < 3))
            def _():
                right(buf, zl - d, c, s_r, recv).wait_send()

            @pl.when((zl + d <= 3) & (zl > 0))
            def _():
                left(buf, zl + d, c, s_l, recv).wait_send()

    def ring_right(o, c):
        return remote(two(gx, c, o), two(gx, c, o), gx_s.at[0, c], gx_r.at[0, c], dev(zh, y, k, (x + 1) % 4, zl))

    def ring_left(o, c):
        return remote(two(gx, c, o), two(gx, c, o), gx_s.at[1, c], gx_r.at[1, c], dev(zh, y, k, (x + 3) % 4, zl))

    def ring_far(to_right, b):
        o, to = ((x + 3) % 4, (x + 1) % 4) if to_right else ((x + 1) % 4, (x + 3) % 4)
        return remote(blk(gx, b, o), blk(gx, b, o), gx_s.at[2, b], gx_r.at[2, b], dev(zh, y, k, to, zl))

    def pair_of(c):
        return (2 * c, 2 * c + 1)

    def g_own(c):
        for b in pair_of(c):
            pltpu.make_async_copy(g_ref.at[0], blk(gz, b, zl), gi_r.at[b]).wait()
        own_line(gz, c, gr_s, gl_s, gz_r)

        @pl.when(source)
        def _():
            pltpu.make_async_copy(two(gz, c, zl), two(gx, c, x), gc_r.at[c]).start()

    def g_pass(c, d):
        pass_line(gz, c, d, gr_s, gl_s, gz_r)

    def x_right(src, o, c, send):
        return remote(src, two(xz, c, o), send, xz_r.at[o, c], at_z((z + 1) % 8))

    def x_left(src, o, c, send):
        return remote(src, two(xz, c, o), send, xz_r.at[o, c], at_z((z + 7) % 8))

    def transit(c, d):
        return remote(xc.at[pl.ds(2 * c, 2)], xt.at[pl.ds(2 * c, 2)], xc_s.at[0, c], xt_r.at[c], at_z((z + d) % 8))

    def x_cross(c):
        @pl.when(zl == 3)
        def _():
            x_right(xc.at[pl.ds(2 * c, 2)], 3, c, xc_s.at[0, c]).start()

        @pl.when(zl == 0)
        def _():
            x_left(xc.at[pl.ds(2 * c, 2)], 0, c, xc_s.at[0, c]).start()

        @pl.when(zl == 2)
        def _():
            transit(c, 1).start()

        @pl.when(zl == 1)
        def _():
            transit(c, 7).start()

    def x_transit(c):
        @pl.when(zl == 3)
        def _():
            transit(c, 1).wait_recv()
            x_right(xt.at[pl.ds(2 * c, 2)], 2, c, xc_s.at[1, c]).start()

        @pl.when(zl == 0)
        def _():
            transit(c, 7).wait_recv()
            x_left(xt.at[pl.ds(2 * c, 2)], 1, c, xc_s.at[1, c]).start()

    def x_own(c):
        @pl.when(source)
        def _():
            for b in pair_of(c):
                pltpu.make_async_copy(x_ref.at[0], blk(xz, b, zl), xa_r.at[b]).wait()
            own_line(xz, c, xr_s, xl_s, xz_r)

    def x_arrive(c, o, to_right):
        if to_right:
            x_right(two(xz, c, o), o, c, xr_s.at[o, c]).wait_recv()

            @pl.when(zl < 3)
            def _():
                x_right(two(xz, c, o), o, c, xr_s.at[o, c]).start()
        else:
            x_left(two(xz, c, o), o, c, xl_s.at[o, c]).wait_recv()

            @pl.when(zl > 0)
            def _():
                x_left(two(xz, c, o), o, c, xl_s.at[o, c]).start()

    def x_start(c):
        @pl.when(source)
        def _():
            for b in pair_of(c):
                pltpu.make_async_copy(x_ref.at[0], xc.at[b], xc_r.at[b]).wait()
            x_cross(c)

    def x_round(c, hops):
        if hops == 1:
            @pl.when(source)
            def _():
                x_transit(c)

        @pl.when(jnp.logical_not(source))
        def _():
            for o, first in ((3, zl + 1), (2, zl + 2), (0, 4 - zl), (1, 5 - zl)):
                @pl.when(first == hops)
                def _():
                    x_arrive(c, o, o >= 2)

    def x_pass(c, d):
        @pl.when(source)
        def _():
            pass_line(xz, c, d, xr_s, xl_s, xz_r)

    def g_cross(near, c):
        o = jnp.where(zl == 3, near, 3 - near)
        return remote(two(gz, c, o), two(gx, c, x), gc_s.at[near, c], gc_r.at[c], dev(1 - zh, y, zh, x, o))

    def g_over(c):
        @pl.when(at_end)
        def _():
            g_cross(0, c).start()
            g_cross(1, c).start()

    def ring_own(c):
        pltpu.make_async_copy(two(gz, c, zl), two(gx, c, x), gc_r.at[c]).wait()
        ring_right(x, c).start()
        ring_left(x, c).start()

    def ring_pass(c):
        even, odd = pair_of(c)
        ring_right((x + 3) % 4, c).wait_recv()
        ring_left((x + 1) % 4, c).wait_recv()
        ring_far(True, even).start()
        ring_far(False, odd).start()

    def ring_end(c):
        even, odd = pair_of(c)
        ring_far(True, even).wait_recv()
        ring_far(False, odd).wait_recv()
        cot = gx[pl.ds(2 * c, 2)]
        gp[pl.ds(2 * c, 2), 0:half] = cot[:, half:]
        gp[pl.ds(2 * c, 2), half:rows] = -cot[:, :half]

    def far(way, c):
        x_ = (x + 2) % 4
        at = pl.ds(0, half) if way == 0 else pl.ds(half, half)
        return remote(
            part.at[x_, pl.ds(2 * c, 2), at], relay.at[way, pl.ds(2 * c, 2)], far_s.at[way, c], far_r.at[way, c],
            dev(zh, y, k, (x + 1 + 2 * way) % 4, zl),
        )

    def near(way, c):
        x_ = (x + 1 + 2 * way) % 4
        return remote(
            part.at[x_, pl.ds(2 * c, 2)], heap.at[way, pl.ds(2 * c, 2)], rs_s.at[way, c], rs_r.at[way, c],
            dev(zh, y, k, x_, zl),
        )

    def back_relay(c):
        for way in (0, 1):
            far(way, c).wait_recv()
            x_ = (x + 1 + 2 * way) % 4
            for b in pair_of(c):
                if way == 0:
                    part[x_, b, 0:half] = part[x_, b, 0:half] + relay[way, b]
                else:
                    part[x_, b, half:rows] = part[x_, b, half:rows] + relay[way, b]
            near(way, c).start()

    def home(b):
        y_, k_ = b // 2, b % 2
        return remote(fin.at[b], back_ref.at[degree], rt_s.at[b], rt_r.at[degree], dev(zh, y_, k_, x, zl))

    def back_reduce(c):
        for way in (0, 1):
            near(way, c).wait_recv()
        for b in pair_of(c):
            fin[b] = part[x, b] + (heap[0, b] + heap[1, b])

            @pl.when(b == me)
            def _():
                pltpu.make_async_copy(fin.at[b], back_ref.at[degree], rt_r.at[degree]).start()

            @pl.when(b != me)
            def _():
                home(b).start()

    def back_product(c):
        cot = gz[pl.ds(2 * c, 2)].reshape(2 * rows, 512)
        over_lanes = (((1,), (1,)), ((), ()))
        by_re = lax.dot_general(cot, wt[0].reshape(512, 512), over_lanes, preferred_element_type=F32)
        by_im = lax.dot_general(cot, wt[1].reshape(512, 512), over_lanes, preferred_element_type=F32)
        for j in range(2):
            lo, mid, hi = j * rows, j * rows + half, (j + 1) * rows
            back_re = by_re[lo:mid] + by_im[mid:hi]
            back_im = by_re[mid:hi] - by_im[lo:mid]
            for x_ in range(NX):
                part[x_, 2 * c + j, 0:half] = back_re[:, x_ * 128 : (x_ + 1) * 128]
                part[x_, 2 * c + j, half:rows] = back_im[:, x_ * 128 : (x_ + 1) * 128]
        for way in (0, 1):
            far(way, c).start()

    def nth(t):
        if t == 0:
            return zl
        if t == 1:
            return zl + 1 - 2 * (zl % 2)
        return jnp.where(zl < 2, t, 3 - t)

    def swap(o):
        return remote(acc.at[1 - k, o], pair.at[o], pair_s.at[o], pair_r.at[o], dev(zh, y, 1 - k, x, zl))

    def owner_rows(o):
        return pl.ds(pl.multiple_of((x % 2) * 512 + o * 128, 128), 128)

    def wgrad_to(d, o):
        return remote(
            acc.at[k, o, :, lanes((x + d) % 4)], wgrad_ref.at[k, owner_rows(o)],
            wo_s.at[d, o], wo_r.at[x % 2, k, o], dev(zh, y, x // 2, (x + d) % 4, zl),
        )

    def wgrad_product(t):
        o = nth(t)

        left_ = xz[:, :, lanes(o)].reshape(NB * rows, 128)
        over_rows = (((0,), (0,)), ((), ()))
        acc[0, o] = lax.dot_general(left_, gx[...].reshape(NB * rows, 512), over_rows, preferred_element_type=F32)
        acc[1, o] = lax.dot_general(left_, gp[...].reshape(NB * rows, 512), over_rows, preferred_element_type=F32)
        swap(o).start()

    def wgrad_send(t):
        o = nth(t)
        swap(o).wait_recv()
        acc[k, o] = acc[k, o] + pair[o]
        for d in (1, 3, 2):
            wgrad_to(d, o).start()

        @pl.when(k == x // 2)
        def _():
            pltpu.make_async_copy(
                acc.at[k, o, :, lanes(x)], wgrad_ref.at[k, owner_rows(o)], wo_r.at[x % 2, k, o]
            ).start()

        @pl.when(k != x // 2)
        def _():
            wgrad_to(0, o).start()

    def when_chunk(c, work):
        @pl.when((c >= 0) & (c < 4))
        def _():
            work(c)

    def pipeline(s, _):
        when_chunk(s, g_own)
        when_chunk(s - 1, x_start)
        when_chunk(s - 1, lambda c: g_pass(c, 1))
        when_chunk(s - 2, lambda c: x_round(c, 1))

        @pl.when(source)
        def _():
            when_chunk(s - 1, ring_own)

        when_chunk(s - 2, lambda c: g_pass(c, 2))
        when_chunk(s - 3, lambda c: x_round(c, 2))

        @pl.when(source)
        def _():
            when_chunk(s - 2, ring_pass)


        @pl.when(s == 3)
        def _():
            w_loc_copy.wait()
            for copy in w_copies:
                copy.wait_recv()

        def product(c):
            g_pass(c, 3)
            g_over(c)
            back_product(c)

        when_chunk(s - 4, back_relay)
        when_chunk(s - 3, product)
        when_chunk(s - 3, x_own)
        when_chunk(s - 4, lambda c: x_round(c, 3))
        when_chunk(s - 5, lambda c: x_round(c, 4))
        @pl.when(source)
        def _():
            when_chunk(s - 3, ring_end)

        @pl.when(jnp.logical_not(source))
        def _():
            when_chunk(s - 4, ring_own)
            when_chunk(s - 5, ring_pass)
            when_chunk(s - 6, ring_end)

        when_chunk(s - 6, lambda c: x_round(c, 5))
        when_chunk(s - 6, back_reduce)
        return 0

    def every(work):
        def step(c, _):
            work(c)
            return 0

        lax.fori_loop(0, 4, step, 0)

    lax.fori_loop(0, 7, pipeline, 0)
    x_round(3, 3)
    x_round(2, 4)
    x_round(1, 5)

    @pl.when(jnp.logical_not(source))
    def _():
        ring_own(3)

    back_relay(3)
    x_round(3, 4)
    x_round(2, 5)
    x_round(3, 5)
    every(lambda c: x_pass(c, 1))

    @pl.when(jnp.logical_not(source))
    def _():
        ring_pass(2)
        ring_end(1)
        ring_pass(3)
        ring_end(2)
        ring_end(3)

    every(lambda c: x_pass(c, 2))
    back_reduce(1)
    wgrad_product(0)
    wgrad_product(1)
    wgrad_send(0)
    wgrad_product(2)
    wgrad_send(1)
    back_reduce(2)
    every(lambda c: x_pass(c, 3))
    wgrad_product(3)
    wgrad_send(2)
    wgrad_send(3)
    back_reduce(3)

    def drain_pairs(c, _):
        @pl.when(source)
        def _():
            drain_line(xz, c, xr_s, xl_s, xz_r)
            x_right(xc.at[pl.ds(2 * c, 2)], 3, c, xc_s.at[0, c]).wait_send()

            @pl.when((zl == 0) | (zl == 3))
            def _():
                x_right(xt.at[pl.ds(2 * c, 2)], 2, c, xc_s.at[1, c]).wait_send()

        @pl.when(jnp.logical_not(source))
        def _():
            for o in (0, 1, 2, 3):
                if o >= 2:
                    @pl.when(zl < 3)
                    def _():
                        x_right(two(xz, c, o), o, c, xr_s.at[o, c]).wait_send()
                else:
                    @pl.when(zl > 0)
                    def _():
                        x_left(two(xz, c, o), o, c, xl_s.at[o, c]).wait_send()

        drain_line(gz, c, gr_s, gl_s, gz_r)
        @pl.when(at_end)
        def _():
            g_cross(0, c).wait_send()
            g_cross(1, c).wait_send()

        ring_right(x, c).wait_send()
        ring_left(x, c).wait_send()
        return 0

    lax.fori_loop(0, 4, drain_pairs, 0)

    def drain(b, _):
        ring_far(True, b).wait_send()

        @pl.when(jnp.logical_or(zh != k, b % 4 != y))
        def _():
            pltpu.make_async_copy(x_ref.at[b], blk(xz, 0, zl), xa_s.at[b]).wait()

        @pl.when(b != me)
        def _():
            pltpu.make_async_copy(g_ref.at[0], blk(gz, 0, zl), gi_s.at[b]).wait()
            home(b).wait_send()

        return 0

    lax.fori_loop(0, NB, drain, 0)

    def drain_scatter(c, _):
        for way in (0, 1):
            far(way, c).wait_send()
            near(way, c).wait_send()
        return 0

    lax.fori_loop(0, NB // 2, drain_scatter, 0)
    for copy in w_copies:
        copy.wait_send()

    def returned(l, _):
        pltpu.make_async_copy(fin.at[0], back_ref.at[l], rt_r.at[l]).wait()
        return 0

    lax.fori_loop(0, NB, returned, 0)

    def owned(o, _):
        swap(o).wait_send()
        for d in (1, 2, 3):
            wgrad_to(d, o).wait_send()

        @pl.when(k != x // 2)
        def _():
            wgrad_to(0, o).wait_send()

        for r in range(2):
            for k_ in range(2):
                at = pl.ds(pl.multiple_of(r * 512 + o * 128, 128), 128)
                pltpu.make_async_copy(acc.at[0, 0, :, pl.ds(0, 128)], wgrad_ref.at[k_, at], wo_r.at[r, k_, o]).wait()
        return 0

    lax.fori_loop(0, NZ, owned, 0)


def per_device(window, inputs, out_grad, weights):
    _, samples, degrees, orders, width = inputs.shape
    step = -(-orders // 16) * 16
    half = samples * step
    rows = 2 * half

    dma, vmem = pltpu.SemaphoreType.DMA, pltpu.VMEM
    back, wgrad = pl.pallas_call(
        functools.partial(kernel, orders, rows),
        name="mix_back",
        out_shape=(
            jax.ShapeDtypeStruct((degrees, rows, width), F32),
            jax.ShapeDtypeStruct((2, 1024, width), F32),
        ),
        in_specs=[
            pl.BlockSpec(memory_space=pltpu.SMEM),
            pl.BlockSpec(memory_space=pl.ANY),
            pl.BlockSpec(memory_space=pl.ANY),
            pl.BlockSpec(memory_space=pl.ANY),
        ],
        out_specs=(pl.BlockSpec(memory_space=pl.ANY), pl.BlockSpec(memory_space=pl.ANY)),
        scratch_shapes=[
            vmem((2, samples, orders, degrees, width), BF16),
            vmem((2, samples, orders, degrees, width), BF16),
            vmem((degrees, rows, width), BF16),
            vmem((degrees, rows, width), BF16),
            vmem((NB, rows, 512), BF16),
            vmem((NB, rows, 128), BF16),
            vmem((NB, rows, 128), BF16),
            vmem((NB, rows, 512), BF16),
            vmem((NB, rows, 512), BF16),
            vmem((NB, rows, 512), BF16),
            vmem((2, 4, 128, 512), BF16),
            vmem((2, NZ, 128, 512), F32),
            vmem((NZ, 128, 512), F32),
            vmem((NX, NB, rows, 128), F32),
            vmem((2, NB, half, 128), F32),
            vmem((2, NB, rows, 128), F32),
            vmem((NB, rows, 128), F32),
            dma((8,)), dma((8,)), dma((8,)), dma((2, 4)), dma((4,)),
            dma((2, 4)), dma((4,)), dma((8,)), dma((8,)), dma((4,)), dma((4,)), dma(()),
            dma((4, 4)), dma((4, 4)), dma((4, 4)), dma((4, 4)), dma((4, 4)), dma((4, 4)), dma((3, 8)), dma((3, 8)),
            dma((4,)), dma((4,)), dma((4, 4)), dma((2, 2, 4)), dma((2, 4)), dma((2, 4)), dma((2, 4)), dma((2, 4)), dma((8,)), dma((8,)), dma((2,)),
        ],
        compiler_params=pltpu.CompilerParams(
            collective_id=0, has_side_effects=True, vmem_limit_bytes=44 * 2**20
        ),
    )(
        window,
        inputs.transpose(0, 1, 3, 2, 4),
        out_grad.transpose(0, 1, 3, 2, 4),
        weights.reshape(2, degrees, 4, 4, 128, width),
    )
    back = back.reshape(degrees, 2, samples, step, width)[:, :, :, :orders]
    return back.transpose(1, 2, 0, 3, 4), wgrad


def solution(mesh):
    placed = (
        P(),
        P(None, None, None, "order", "chan"),
        P(None, None, None, "order", "chan"),
        P(None, None, "chan"),
    )
    return jax.shard_map(
        per_device,
        mesh=mesh,
        in_specs=placed,
        out_specs=(P(None, None, None, "order", "chan"), P(None, "order", "chan")),
        check_vma=False,
    )
```

```python
import functools

import jax
import jax.numpy as jnp
from jax import lax
from jax.experimental import pallas as pl
from jax.experimental.pallas import tpu as pltpu
from jax.sharding import PartitionSpec as P

MESH = pl.DeviceIdType.MESH
BF16, F32 = jnp.bfloat16, jnp.float32

NX, NY, NZ = 4, 4, 4
NB = 8


def coords():
    order, chan = lax.axis_index("order"), lax.axis_index("chan")
    return order // 8, (order // 2) % 4, order % 2, chan // 4, chan % 4


def lanes(block):
    return pl.ds(pl.multiple_of(block * 128, 128), 128)


def kernel(
    orders, rows, window_ref, x_hbm, g_hbm, w_ref, back_ref, wgrad_ref,
    x_in, g_in, x_ref, g_ref, xz, xc, xt, gx, gp, gz, wt, acc, pair, part, relay, heap, fin,
    xa_s, xa_r, xc_r, xc_s, xt_r, gc_s, gc_r, gi_s, gi_r, w_s, w_r, w_loc,
    xr_s, xl_s, xz_r, gr_s, gl_s, gz_r, gx_s, gx_r,
    pair_s, pair_r, wo_s, wo_r, far_s, far_r, np_s, np_r, rs_s, rs_r, rt_s, rt_r, in_s,
):
    zh, y, k, x, zl = coords()
    z = zh * 4 + zl
    half = rows // 2
    me = y * 2 + k

    def dev(zh_, y_, k_, x_, zl_):
        return (zh_ * 8 + y_ * 2 + k_, x_ * 4 + zl_)

    def at_z(z_):
        return dev(z_ // 4, y, k, x, z_ % 4)

    def greet(device):
        pl.semaphore_signal(pltpu.get_barrier_semaphore(), inc=1, device_id=device, device_id_type=MESH)

    x_load = pltpu.make_async_copy(x_hbm, x_in, in_s.at[0])
    g_load = pltpu.make_async_copy(g_hbm, g_in, in_s.at[1])
    g_load.start()
    x_load.start()

    def greet_half(t, _):
        greet((zh * 8 + (me + t) % 8, x * 4 + zl))
        return 0

    lax.fori_loop(1, 8, greet_half, 0)

    @pl.when(zh != k)
    def _():
        end = jnp.where(zl < 2, 7 - zl, 4 - zl)
        z_ = (z + end) % 8
        greet(dev(z_ // 4, y, 1 - k, x, z_ % 4))

    for d in (1, 2, 6, 7):
        greet(at_z((z + d) % 8))
    for d in (1, 2, 3):
        for other in (0, 1):
            greet(dev(zh, y, other, (x + d) % 4, zl))

    def by_degree(raw, out):
        step = half // raw.shape[1]
        shape = (raw.shape[3], raw.shape[2], 128)
        degree_of = window_ref[0] + lax.broadcasted_iota(jnp.int32, shape, 0)
        order_of = (zh * 8 + me) * orders + lax.broadcasted_iota(jnp.int32, shape, 1)
        live = jnp.where(order_of <= degree_of, 1.0, 0.0)
        pad = jnp.zeros((shape[0], step - shape[1], 128), F32)
        for part_ in range(raw.shape[0]):
            for sample in range(raw.shape[1]):
                values = jnp.swapaxes(raw[part_, sample].astype(F32), 0, 1) * live
                at = pl.ds(part_ * half + sample * step, step)
                out[:, at] = jnp.concatenate([values, pad], axis=1).astype(BF16)

    g_load.wait()
    by_degree(g_in, g_ref)
    x_load.wait()
    by_degree(x_in, x_ref)
    at_end = jnp.logical_and(zh != k, jnp.logical_or(zl == 0, zl == 3))

    @pl.when(at_end)
    def _():
        pl.semaphore_wait(pltpu.get_barrier_semaphore(), 7 + 4 + 6 + 2)

    @pl.when(jnp.logical_not(at_end))
    def _():
        pl.semaphore_wait(pltpu.get_barrier_semaphore(), 7 + 4 + 6)


    def remote(src, dst, send, recv, device):
        return pltpu.make_async_remote_copy(
            src_ref=src, dst_ref=dst, send_sem=send, recv_sem=recv, device_id=device, device_id_type=MESH
        )

    def blk(buf, b, lane):
        return buf.at[b, :, lanes(lane)]

    def two(buf, c, lane):
        return buf.at[pl.ds(2 * c, 2), :, lanes(lane)]

    def to_input(t):
        j = (me + t) % 8
        y_, k_ = j // 2, j % 2
        return remote(g_ref.at[4 * k_ + y_], blk(gz, me, zl), gi_s.at[j], gi_r.at[me], dev(zh, y_, k_, x, zl))

    def gi_step(t, _):
        to_input(t).start()
        return 0

    lax.fori_loop(1, 8, gi_step, 0)
    degree = 4 * k + y
    pltpu.make_async_copy(g_ref.at[degree], blk(gz, me, zl), gi_r.at[me]).start()
    w_loc_copy = pltpu.make_async_copy(w_ref.at[:, degree, :, zl], wt.at[:, :, :, lanes(zl)], w_loc)
    w_loc_copy.start()
    w_copies = []
    for i, (d, part_of) in enumerate(((1, (0, 2)), (7, (0, 2)), (2, (0, 1)), (6, (1, 1)))):
        to = (z + d) % 8
        reim = pl.ds(*part_of)
        w_copies.append(
            remote(w_ref.at[reim, degree, :, to % 4], wt.at[reim, :, :, lanes(zl)], w_s.at[i], w_r.at[i], at_z(to))
        )
        w_copies[-1].start()

    source = zh == k

    def x_out(t, _):
        y_ = (y + t) % 4
        mine, other = zh * 4 + y_, (1 - zh) * 4 + y_
        itself = jnp.logical_and(source, t == 0)

        @pl.when(itself)
        def _():
            pltpu.make_async_copy(x_ref.at[mine], blk(xz, me, zl), xa_r.at[me]).start()
            pltpu.make_async_copy(x_ref.at[other], xc.at[me], xc_r.at[me]).start()

        @pl.when(jnp.logical_not(itself))
        def _():
            to = dev(zh, y_, zh, x, zl)
            remote(x_ref.at[mine], blk(xz, me, zl), xa_s.at[mine], xa_r.at[me], to).start()
            remote(x_ref.at[other], xc.at[me], xa_s.at[other], xc_r.at[me], to).start()

        return 0

    lax.fori_loop(0, 4, x_out, 0)


    def right(buf, o, c, send, recv):
        return remote(two(buf, c, o), two(buf, c, o), send.at[o, c], recv.at[o, c], dev(zh, y, k, x, (zl + 1) % 4))

    def left(buf, o, c, send, recv):
        return remote(two(buf, c, o), two(buf, c, o), send.at[o, c], recv.at[o, c], dev(zh, y, k, x, (zl + 3) % 4))

    def own_line(buf, c, s_r, s_l, recv):
        @pl.when(zl < 3)
        def _():
            right(buf, zl, c, s_r, recv).start()

        @pl.when(zl > 0)
        def _():
            left(buf, zl, c, s_l, recv).start()

    def pass_line(buf, c, d, s_r, s_l, recv):
        @pl.when(zl >= d)
        def _():
            o = zl - d
            right(buf, o, c, s_r, recv).wait_recv()

            @pl.when(zl < 3)
            def _():
                right(buf, o, c, s_r, recv).start()

        @pl.when(zl + d <= 3)
        def _():
            o = zl + d
            left(buf, o, c, s_l, recv).wait_recv()

            @pl.when(zl > 0)
            def _():
                left(buf, o, c, s_l, recv).start()

    def drain_line(buf, c, s_r, s_l, recv):
        for d in range(3):
            @pl.when((zl >= d) & (zl < 3))
            def _():
                right(buf, zl - d, c, s_r, recv).wait_send()

            @pl.when((zl + d <= 3) & (zl > 0))
            def _():
                left(buf, zl + d, c, s_l, recv).wait_send()

    def ring_right(o, c):
        return remote(two(gx, c, o), two(gx, c, o), gx_s.at[0, c], gx_r.at[0, c], dev(zh, y, k, (x + 1) % 4, zl))

    def ring_left(o, c):
        return remote(two(gx, c, o), two(gx, c, o), gx_s.at[1, c], gx_r.at[1, c], dev(zh, y, k, (x + 3) % 4, zl))

    def ring_far(to_right, b):
        o, to = ((x + 3) % 4, (x + 1) % 4) if to_right else ((x + 1) % 4, (x + 3) % 4)
        return remote(blk(gx, b, o), blk(gx, b, o), gx_s.at[2, b], gx_r.at[2, b], dev(zh, y, k, to, zl))

    def pair_of(c):
        return (2 * c, 2 * c + 1)

    def g_own(c):
        for b in pair_of(c):
            pltpu.make_async_copy(g_ref.at[0], blk(gz, b, zl), gi_r.at[b]).wait()
        own_line(gz, c, gr_s, gl_s, gz_r)

        @pl.when(source)
        def _():
            pltpu.make_async_copy(two(gz, c, zl), two(gx, c, x), gc_r.at[c]).start()

    def g_pass(c, d):
        pass_line(gz, c, d, gr_s, gl_s, gz_r)

    def x_right(src, o, c, send):
        return remote(src, two(xz, c, o), send, xz_r.at[o, c], at_z((z + 1) % 8))

    def x_left(src, o, c, send):
        return remote(src, two(xz, c, o), send, xz_r.at[o, c], at_z((z + 7) % 8))

    def transit(c, d):
        return remote(xc.at[pl.ds(2 * c, 2)], xt.at[pl.ds(2 * c, 2)], xc_s.at[0, c], xt_r.at[c], at_z((z + d) % 8))

    def x_cross(c):
        @pl.when(zl == 3)
        def _():
            x_right(xc.at[pl.ds(2 * c, 2)], 3, c, xc_s.at[0, c]).start()

        @pl.when(zl == 0)
        def _():
            x_left(xc.at[pl.ds(2 * c, 2)], 0, c, xc_s.at[0, c]).start()

        @pl.when(zl == 2)
        def _():
            transit(c, 1).start()

        @pl.when(zl == 1)
        def _():
            transit(c, 7).start()

    def x_transit(c):
        @pl.when(zl == 3)
        def _():
            transit(c, 1).wait_recv()
            x_right(xt.at[pl.ds(2 * c, 2)], 2, c, xc_s.at[1, c]).start()

        @pl.when(zl == 0)
        def _():
            transit(c, 7).wait_recv()
            x_left(xt.at[pl.ds(2 * c, 2)], 1, c, xc_s.at[1, c]).start()

    def x_own(c):
        @pl.when(source)
        def _():
            for b in pair_of(c):
                pltpu.make_async_copy(x_ref.at[0], blk(xz, b, zl), xa_r.at[b]).wait()
            own_line(xz, c, xr_s, xl_s, xz_r)

    def x_arrive(c, o, to_right):
        if to_right:
            x_right(two(xz, c, o), o, c, xr_s.at[o, c]).wait_recv()

            @pl.when(zl < 3)
            def _():
                x_right(two(xz, c, o), o, c, xr_s.at[o, c]).start()
        else:
            x_left(two(xz, c, o), o, c, xl_s.at[o, c]).wait_recv()

            @pl.when(zl > 0)
            def _():
                x_left(two(xz, c, o), o, c, xl_s.at[o, c]).start()

    def x_start(c):
        @pl.when(source)
        def _():
            for b in pair_of(c):
                pltpu.make_async_copy(x_ref.at[0], xc.at[b], xc_r.at[b]).wait()
            x_cross(c)

    def x_round(c, hops):
        if hops == 1:
            @pl.when(source)
            def _():
                x_transit(c)

        @pl.when(jnp.logical_not(source))
        def _():
            for o, first in ((3, zl + 1), (2, zl + 2), (0, 4 - zl), (1, 5 - zl)):
                @pl.when(first == hops)
                def _():
                    x_arrive(c, o, o >= 2)

    def x_pass(c, d):
        @pl.when(source)
        def _():
            pass_line(xz, c, d, xr_s, xl_s, xz_r)

    def g_cross(near, c):
        o = jnp.where(zl == 3, near, 3 - near)
        return remote(two(gz, c, o), two(gx, c, x), gc_s.at[near, c], gc_r.at[c], dev(1 - zh, y, zh, x, o))

    def g_over(c):
        @pl.when(at_end)
        def _():
            g_cross(0, c).start()
            g_cross(1, c).start()

    def ring_own(c):
        pltpu.make_async_copy(two(gz, c, zl), two(gx, c, x), gc_r.at[c]).wait()
        ring_right(x, c).start()
        ring_left(x, c).start()

    def ring_pass(c):
        even, odd = pair_of(c)
        ring_right((x + 3) % 4, c).wait_recv()
        ring_left((x + 1) % 4, c).wait_recv()
        ring_far(True, even).start()
        ring_far(False, odd).start()

    def ring_end(c):
        even, odd = pair_of(c)
        ring_far(True, even).wait_recv()
        ring_far(False, odd).wait_recv()
        cot = gx[pl.ds(2 * c, 2)]
        gp[pl.ds(2 * c, 2), 0:half] = cot[:, half:]
        gp[pl.ds(2 * c, 2), half:rows] = -cot[:, :half]

    def far(way, c):
        x_ = (x + 2) % 4
        at = pl.ds(0, half) if way == 0 else pl.ds(half, half)
        return remote(
            part.at[x_, pl.ds(2 * c, 2), at], relay.at[way, pl.ds(2 * c, 2)], far_s.at[way, c], far_r.at[way, c],
            dev(zh, y, k, (x + 1 + 2 * way) % 4, zl),
        )

    def near(way, c, added):
        x_ = (x + 1 + 2 * way) % 4
        at = pl.ds(0, half) if (way == 0) == added else pl.ds(half, half)
        send, recv = (rs_s, rs_r) if added else (np_s, np_r)
        return remote(
            part.at[x_, pl.ds(2 * c, 2), at], heap.at[way, pl.ds(2 * c, 2), at], send.at[way, c], recv.at[way, c],
            dev(zh, y, k, x_, zl),
        )

    def back_relay(c):
        for way in (0, 1):
            far(way, c).wait_recv()
            x_ = (x + 1 + 2 * way) % 4
            for b in pair_of(c):
                if way == 0:
                    part[x_, b, 0:half] = part[x_, b, 0:half] + relay[way, b]
                else:
                    part[x_, b, half:rows] = part[x_, b, half:rows] + relay[way, b]
            near(way, c, True).start()

    def home(b):
        y_, k_ = b // 2, b % 2
        return remote(fin.at[b], back_ref.at[degree], rt_s.at[b], rt_r.at[degree], dev(zh, y_, k_, x, zl))

    def back_reduce(c):
        for way in (0, 1):
            near(way, c, False).wait_recv()
            near(way, c, True).wait_recv()
        for b in pair_of(c):
            fin[b] = part[x, b] + (heap[0, b] + heap[1, b])

            @pl.when(b == me)
            def _():
                pltpu.make_async_copy(fin.at[b], back_ref.at[degree], rt_r.at[degree]).start()

            @pl.when(b != me)
            def _():
                home(b).start()

    def back_product(c):
        cot = gz[pl.ds(2 * c, 2)].reshape(2 * rows, 512)
        over_lanes = (((1,), (1,)), ((), ()))
        by_re = lax.dot_general(cot, wt[0].reshape(512, 512), over_lanes, preferred_element_type=F32)
        by_im = lax.dot_general(cot, wt[1].reshape(512, 512), over_lanes, preferred_element_type=F32)
        for j in range(2):
            lo, mid, hi = j * rows, j * rows + half, (j + 1) * rows
            back_re = by_re[lo:mid] + by_im[mid:hi]
            back_im = by_re[mid:hi] - by_im[lo:mid]
            for x_ in range(NX):
                part[x_, 2 * c + j, 0:half] = back_re[:, x_ * 128 : (x_ + 1) * 128]
                part[x_, 2 * c + j, half:rows] = back_im[:, x_ * 128 : (x_ + 1) * 128]
        for way in (0, 1):
            far(way, c).start()
        for way in (0, 1):
            near(way, c, False).start()

    def nth(t):
        if t == 0:
            return zl
        if t == 1:
            return zl + 1 - 2 * (zl % 2)
        return jnp.where(zl < 2, t, 3 - t)

    def swap(o):
        return remote(acc.at[1 - k, o], pair.at[o], pair_s.at[o], pair_r.at[o], dev(zh, y, 1 - k, x, zl))

    def owner_rows(o):
        return pl.ds(pl.multiple_of((x % 2) * 512 + o * 128, 128), 128)

    def wgrad_to(d, o):
        return remote(
            acc.at[k, o, :, lanes((x + d) % 4)], wgrad_ref.at[k, owner_rows(o)],
            wo_s.at[d, o], wo_r.at[x % 2, k, o], dev(zh, y, x // 2, (x + d) % 4, zl),
        )

    def wgrad_product(t):
        o = nth(t)

        left_ = xz[:, :, lanes(o)].reshape(NB * rows, 128)
        over_rows = (((0,), (0,)), ((), ()))
        acc[0, o] = lax.dot_general(left_, gx[...].reshape(NB * rows, 512), over_rows, preferred_element_type=F32)
        acc[1, o] = lax.dot_general(left_, gp[...].reshape(NB * rows, 512), over_rows, preferred_element_type=F32)
        swap(o).start()

    def wgrad_send(t):
        o = nth(t)
        swap(o).wait_recv()
        acc[k, o] = acc[k, o] + pair[o]
        for d in (1, 3, 2):
            wgrad_to(d, o).start()

        @pl.when(k == x // 2)
        def _():
            pltpu.make_async_copy(
                acc.at[k, o, :, lanes(x)], wgrad_ref.at[k, owner_rows(o)], wo_r.at[x % 2, k, o]
            ).start()

        @pl.when(k != x // 2)
        def _():
            wgrad_to(0, o).start()

    def when_chunk(c, work):
        @pl.when((c >= 0) & (c < 4))
        def _():
            work(c)

    def pipeline(s, _):
        when_chunk(s, g_own)
        when_chunk(s - 1, x_start)
        when_chunk(s - 1, lambda c: g_pass(c, 1))
        when_chunk(s - 2, lambda c: x_round(c, 1))

        @pl.when(source)
        def _():
            when_chunk(s - 1, ring_own)

        when_chunk(s - 2, lambda c: g_pass(c, 2))
        when_chunk(s - 3, lambda c: x_round(c, 2))

        @pl.when(source)
        def _():
            when_chunk(s - 2, ring_pass)


        @pl.when(s == 3)
        def _():
            w_loc_copy.wait()
            for copy in w_copies:
                copy.wait_recv()

        def product(c):
            g_pass(c, 3)
            g_over(c)
            back_product(c)

        when_chunk(s - 4, back_relay)
        when_chunk(s - 3, product)
        when_chunk(s - 3, x_own)
        when_chunk(s - 4, lambda c: x_round(c, 3))
        when_chunk(s - 5, lambda c: x_round(c, 4))
        @pl.when(source)
        def _():
            when_chunk(s - 3, ring_end)

        @pl.when(jnp.logical_not(source))
        def _():
            when_chunk(s - 4, ring_own)
            when_chunk(s - 5, ring_pass)
            when_chunk(s - 6, ring_end)

        when_chunk(s - 6, lambda c: x_round(c, 5))
        when_chunk(s - 6, back_reduce)
        return 0

    def every(work):
        def step(c, _):
            work(c)
            return 0

        lax.fori_loop(0, 4, step, 0)

    lax.fori_loop(0, 7, pipeline, 0)
    x_round(3, 3)
    x_round(2, 4)
    x_round(1, 5)

    @pl.when(jnp.logical_not(source))
    def _():
        ring_own(3)

    back_relay(3)
    x_round(3, 4)
    x_round(2, 5)
    x_round(3, 5)
    every(lambda c: x_pass(c, 1))
    every(lambda c: x_pass(c, 2))

    @pl.when(jnp.logical_not(source))
    def _():
        ring_pass(2)
        ring_end(1)
        ring_pass(3)
        ring_end(2)
        ring_end(3)

    wgrad_product(0)
    back_reduce(1)
    wgrad_product(1)
    wgrad_send(0)
    wgrad_product(2)
    wgrad_send(1)
    back_reduce(2)
    every(lambda c: x_pass(c, 3))
    wgrad_product(3)
    wgrad_send(2)
    wgrad_send(3)
    back_reduce(3)

    def drain_pairs(c, _):
        @pl.when(source)
        def _():
            drain_line(xz, c, xr_s, xl_s, xz_r)
            x_right(xc.at[pl.ds(2 * c, 2)], 3, c, xc_s.at[0, c]).wait_send()

            @pl.when((zl == 0) | (zl == 3))
            def _():
                x_right(xt.at[pl.ds(2 * c, 2)], 2, c, xc_s.at[1, c]).wait_send()

        @pl.when(jnp.logical_not(source))
        def _():
            for o in (0, 1, 2, 3):
                if o >= 2:
                    @pl.when(zl < 3)
                    def _():
                        x_right(two(xz, c, o), o, c, xr_s.at[o, c]).wait_send()
                else:
                    @pl.when(zl > 0)
                    def _():
                        x_left(two(xz, c, o), o, c, xl_s.at[o, c]).wait_send()

        drain_line(gz, c, gr_s, gl_s, gz_r)
        @pl.when(at_end)
        def _():
            g_cross(0, c).wait_send()
            g_cross(1, c).wait_send()

        ring_right(x, c).wait_send()
        ring_left(x, c).wait_send()
        return 0

    lax.fori_loop(0, 4, drain_pairs, 0)

    def drain(b, _):
        ring_far(True, b).wait_send()

        @pl.when(jnp.logical_or(zh != k, b % 4 != y))
        def _():
            pltpu.make_async_copy(x_ref.at[b], blk(xz, 0, zl), xa_s.at[b]).wait()

        @pl.when(b != me)
        def _():
            pltpu.make_async_copy(g_ref.at[0], blk(gz, 0, zl), gi_s.at[b]).wait()
            home(b).wait_send()

        return 0

    lax.fori_loop(0, NB, drain, 0)

    def drain_scatter(c, _):
        for way in (0, 1):
            far(way, c).wait_send()
            near(way, c, False).wait_send()
            near(way, c, True).wait_send()
        return 0

    lax.fori_loop(0, NB // 2, drain_scatter, 0)
    for copy in w_copies:
        copy.wait_send()

    def returned(l, _):
        pltpu.make_async_copy(fin.at[0], back_ref.at[l], rt_r.at[l]).wait()
        return 0

    lax.fori_loop(0, NB, returned, 0)

    def owned(o, _):
        swap(o).wait_send()
        for d in (1, 2, 3):
            wgrad_to(d, o).wait_send()

        @pl.when(k != x // 2)
        def _():
            wgrad_to(0, o).wait_send()

        for r in range(2):
            for k_ in range(2):
                at = pl.ds(pl.multiple_of(r * 512 + o * 128, 128), 128)
                pltpu.make_async_copy(acc.at[0, 0, :, pl.ds(0, 128)], wgrad_ref.at[k_, at], wo_r.at[r, k_, o]).wait()
        return 0

    lax.fori_loop(0, NZ, owned, 0)


def per_device(window, inputs, out_grad, weights):
    _, samples, degrees, orders, width = inputs.shape
    step = -(-orders // 16) * 16
    half = samples * step
    rows = 2 * half

    dma, vmem = pltpu.SemaphoreType.DMA, pltpu.VMEM
    back, wgrad = pl.pallas_call(
        functools.partial(kernel, orders, rows),
        name="mix_back",
        out_shape=(
            jax.ShapeDtypeStruct((degrees, rows, width), F32),
            jax.ShapeDtypeStruct((2, 1024, width), F32),
        ),
        in_specs=[
            pl.BlockSpec(memory_space=pltpu.SMEM),
            pl.BlockSpec(memory_space=pl.ANY),
            pl.BlockSpec(memory_space=pl.ANY),
            pl.BlockSpec(memory_space=pl.ANY),
        ],
        out_specs=(pl.BlockSpec(memory_space=pl.ANY), pl.BlockSpec(memory_space=pl.ANY)),
        scratch_shapes=[
            vmem((2, samples, orders, degrees, width), BF16),
            vmem((2, samples, orders, degrees, width), BF16),
            vmem((degrees, rows, width), BF16),
            vmem((degrees, rows, width), BF16),
            vmem((NB, rows, 512), BF16),
            vmem((NB, rows, 128), BF16),
            vmem((NB, rows, 128), BF16),
            vmem((NB, rows, 512), BF16),
            vmem((NB, rows, 512), BF16),
            vmem((NB, rows, 512), BF16),
            vmem((2, 4, 128, 512), BF16),
            vmem((2, NZ, 128, 512), F32),
            vmem((NZ, 128, 512), F32),
            vmem((NX, NB, rows, 128), F32),
            vmem((2, NB, half, 128), F32),
            vmem((2, NB, rows, 128), F32),
            vmem((NB, rows, 128), F32),
            dma((8,)), dma((8,)), dma((8,)), dma((2, 4)), dma((4,)),
            dma((2, 4)), dma((4,)), dma((8,)), dma((8,)), dma((4,)), dma((4,)), dma(()),
            dma((4, 4)), dma((4, 4)), dma((4, 4)), dma((4, 4)), dma((4, 4)), dma((4, 4)), dma((3, 8)), dma((3, 8)),
            dma((4,)), dma((4,)), dma((4, 4)), dma((2, 2, 4)), dma((2, 4)), dma((2, 4)), dma((2, 4)), dma((2, 4)), dma((2, 4)), dma((2, 4)), dma((8,)), dma((8,)), dma((2,)),
        ],
        compiler_params=pltpu.CompilerParams(
            collective_id=0, has_side_effects=True, vmem_limit_bytes=44 * 2**20
        ),
    )(
        window,
        inputs.transpose(0, 1, 3, 2, 4),
        out_grad.transpose(0, 1, 3, 2, 4),
        weights.reshape(2, degrees, 4, 4, 128, width),
    )
    back = back.reshape(degrees, 2, samples, step, width)[:, :, :, :orders]
    return back.transpose(1, 2, 0, 3, 4), wgrad


def solution(mesh):
    placed = (
        P(),
        P(None, None, None, "order", "chan"),
        P(None, None, None, "order", "chan"),
        P(None, None, "chan"),
    )
    return jax.shard_map(
        per_device,
        mesh=mesh,
        in_specs=placed,
        out_specs=(P(None, None, None, "order", "chan"), P(None, "order", "chan")),
        check_vma=False,
    )
```
